32 devices in a mesh: grp: 4 (over y, core), pair: 8 (over z, x).
Axes of the slice: x: 2, y: 2, z: 4, core: 2. Of those that a mesh axis runs over, the one named last changes fastest.
Arguments:
- integrals: bfloat16 [64, 2000, 2000], P('pair', 'grp'), may hold values from -6 to 6
- coeff: bfloat16 [2000, 96], replicated, may hold values from -0.125 to 0.125
- mu_index: int32 [64], replicated, may hold values from 0 to 1999
- nu_index: int32 [64], replicated, may hold values from 0 to 7
- ao_irrep: int32 [8], replicated, may hold values from 0 to 7
- act_irrep: int32 [96], replicated, may hold values from 0 to 7
Outputs:
- transformed: float32 [9216, 768], P(('grp', 'pair'))
The draws below stay inside these ranges and needn't reach their ends.
All inputs are finite; a program needn't handle non-finite values.
Results may differ from the reference program's by a relative error of at most 0.0029.
Values sent between devices are 32-bit elements; how exact they have to be, the bound alone decides.
A program may use at most 128 MiB of HBM per device.

```python
import jax
import jax.numpy as jnp
from jax import lax

NBF = 2000
NACT = 96
NNU = 8
ROWS = 64


def place_ends(values, own_key, smallest, largest):
    longest = values.shape.index(max(values.shape))
    spots = []
    for shift in (0, 1):
        where = [jax.random.randint(jax.random.fold_in(own_key, axis), (), 0, length) for axis, length in enumerate(values.shape)]
        where[longest] = (where[longest] + shift) % values.shape[longest]
        spots.append(tuple(where))
    return values.at[spots[0]].set(smallest).at[spots[1]].set(largest)


def steps_of(rng, extent, cuts, least, high):
    level, own = 1.0, jax.random.fold_in(rng, 6)
    for position, parts in cuts:
        draws = jnp.exp(jax.random.uniform(jax.random.fold_in(own, position), (parts,), jnp.float32, least / len(cuts), high / len(cuts)))
        level = level * jnp.repeat(draws, extent[position] // parts).reshape([-1 if axis == position else 1 for axis in range(len(extent))])
    return level


def scatter_about(stream_key, extent, width, reach, cuts=(), kind=jnp.bfloat16):
    level = steps_of(stream_key, extent, cuts, -0.22, 0.18) if cuts else 1.0
    array = jax.random.normal(stream_key, extent, jnp.float32) * width * level
    return jnp.minimum(jnp.maximum(array, -reach), reach).astype(kind)


def setup_inputs(seed: int = 0) -> dict:
    streams_of = jax.random.split(jax.random.key(seed), 7)
    integrals = scatter_about(streams_of[0], (ROWS, NBF, NBF), 1.0, 6.0, ((0, 8), (1, 4)))
    coeff = scatter_about(streams_of[1], (NBF, NACT), NBF ** -0.5, 0.125)
    mu_index = place_ends(jax.random.randint(streams_of[2], (ROWS,), 0, NBF), jax.random.fold_in(streams_of[2], 1), 0, NBF - 1).astype(jnp.int32)
    nu_index = place_ends(jax.random.randint(streams_of[3], (ROWS,), 0, NNU), jax.random.fold_in(streams_of[3], 1), 0, NNU - 1).astype(jnp.int32)
    ao_irrep = place_ends(jax.random.randint(streams_of[4], (NNU,), 0, 8), jax.random.fold_in(streams_of[4], 1), 0, 7).astype(jnp.int32)
    act_irrep = place_ends(jax.random.randint(streams_of[5], (NACT,), 0, 8), jax.random.fold_in(streams_of[5], 1), 0, 7).astype(jnp.int32)
    return dict(integrals=integrals, coeff=coeff, mu_index=mu_index, nu_index=nu_index, ao_irrep=ao_irrep, act_irrep=act_irrep)


def reference(integrals, coeff, mu_index, nu_index, ao_irrep, act_irrep):
    def half_row(row):
        quarter = jnp.dot(row, coeff, preferred_element_type=jnp.float32).astype(jnp.bfloat16)
        return jnp.dot(coeff.T, quarter, preferred_element_type=jnp.float32)

    halves = lax.map(half_row, integrals)
    half = halves.reshape(ROWS, NACT * NACT).T
    picked = coeff[mu_index].astype(jnp.float32)
    onehot = (nu_index[:, None] == jnp.arange(NNU, dtype=jnp.int32)[None, :]).astype(jnp.float32)
    amat = (onehot[:, :, None] * picked[:, None, :]).reshape(ROWS, NNU * NACT)
    full = jnp.dot(half, amat, precision=lax.Precision.HIGHEST)
    pair_ids = jnp.arange(NACT * NACT, dtype=jnp.int32)
    left_irrep = jnp.bitwise_xor(act_irrep[pair_ids // NACT], act_irrep[pair_ids % NACT])
    col_ids = jnp.arange(NNU * NACT, dtype=jnp.int32)
    right_irrep = jnp.bitwise_xor(ao_irrep[col_ids // NACT], act_irrep[col_ids % NACT])
    allowed = left_irrep[:, None] == right_irrep[None, :]
    return jnp.where(allowed, full, jnp.zeros_like(full))
```

```python
import functools

import jax
import jax.numpy as jnp
from jax import lax
from jax.experimental import pallas as pl
from jax.experimental.pallas import tpu as pltpu
from jax.sharding import PartitionSpec as P

MESH = pl.DeviceIdType.MESH
F32 = jnp.float32
BF16 = jnp.bfloat16
LANES = 128


def generic(integrals, coeff, mu_index, nu_index, ao_irrep, act_irrep):
    rows_dev, slab, nbasis = integrals.shape
    nactive = coeff.shape[1]
    groups = lax.axis_size("grp")
    owners = lax.axis_size("pair")
    total = nactive * nactive
    share = total // groups
    subset = share // owners
    all_rows = mu_index.shape[0]
    nsecond = ao_irrep.shape[0]
    slab_coeff = lax.dynamic_slice_in_dim(coeff, lax.axis_index("grp") * slab, slab, 0)
    rows_first = integrals.transpose(1, 0, 2).reshape(slab * rows_dev, nbasis)
    quarter = jnp.dot(rows_first, coeff, preferred_element_type=F32)
    quarter = quarter.astype(BF16).reshape(slab, rows_dev, nactive)
    partial_value = jnp.einsum("lp,lrq->rpq", slab_coeff, quarter, preferred_element_type=F32)
    partial_value = partial_value.reshape(rows_dev, total)
    mine = lax.psum_scatter(partial_value, "grp", scatter_dimension=1, tiled=True)
    picked = jnp.take(coeff, mu_index, axis=0).astype(F32)
    onehot = (nu_index[:, None] == jnp.arange(nsecond, dtype=jnp.int32)[None, :]).astype(F32)
    amat = (onehot[:, :, None] * picked[:, None, :]).reshape(all_rows, nsecond * nactive)
    sectioned = mine.reshape(rows_dev, owners, subset)
    arrived = lax.all_to_all(sectioned, "pair", split_axis=1, concat_axis=0, tiled=True)
    flat = arrived.reshape(all_rows, arrived.shape[2])
    full = lax.dot_general(flat, amat, (((0,), (0,)), ((), ())), precision=lax.Precision.HIGHEST)
    block_id = lax.axis_index("grp") * owners + lax.axis_index("pair")
    pair_ids = block_id * subset + jnp.arange(subset, dtype=jnp.int32)
    left_irrep = jnp.bitwise_xor(
        jnp.take(act_irrep, pair_ids // nactive), jnp.take(act_irrep, pair_ids % nactive)
    )
    col_ids = jnp.arange(nsecond * nactive, dtype=jnp.int32)
    right_irrep = jnp.bitwise_xor(
        jnp.take(ao_irrep, col_ids // nactive), jnp.take(act_irrep, col_ids % nactive)
    )
    allowed = left_irrep[:, None] == right_irrep[None, :]
    return jnp.where(allowed, full, jnp.zeros_like(full))


def as_column(row, n):
    eye = lax.broadcasted_iota(jnp.int32, (n, n), 0) == lax.broadcasted_iota(jnp.int32, (n, n), 1)
    return jnp.sum(jnp.where(eye, jnp.broadcast_to(row, (n, n)), 0.0), axis=1, keepdims=True)


def section_of(shape, nactive, nsecond):
    col = lax.broadcasted_iota(jnp.int32, shape, 1)
    section = jnp.zeros(shape, jnp.int32)
    for n in range(1, nsecond):
        section = section + jnp.where(col >= n * nactive, 1, 0)
    return section


def transform_kernel(
    dims, x_hbm, c_hbm, mu_hbm, nu_hbm, ao_hbm, act_hbm, flat_ref, amat_ref, right_ref, actcol_ref,
    xv, cv, cpad, c32, qv, pv, muv, nuv, aov, actv, from_core, kept, from_y, summed, flat,
    x_sem, in_sem, core_send, core_recv, y_send, y_recv, pair_send, pair_recv,
):
    groups, owners, slab, rows_dev, nbasis, nact, nsecond, all_rows, chunk, early = dims
    layers = groups // 2
    per_group = nact // groups
    per_owner = per_group // owners
    grows = per_group * rows_dev
    orows = per_owner * rows_dev
    g = lax.axis_index("grp")
    me = lax.axis_index("pair")
    y, core = g // 2, g % 2
    other = 1 - core
    nchunks = slab * rows_dev // chunk

    small = [
        pltpu.make_async_copy(src, dst, in_sem.at[k])
        for k, (src, dst) in enumerate(
            ((c_hbm, cv), (mu_hbm, muv), (nu_hbm, nuv), (ao_hbm, aov), (act_hbm, actv))
        )
    ]
    small[0].start()

    def x_copy(k):
        where = pl.ds(pl.multiple_of(k * chunk, 16), chunk)
        return pltpu.make_async_copy(x_hbm.at[where, :], xv.at[where, :], x_sem.at[k])

    for k in range(nchunks):
        x_copy(k).start()
    for copy in small[1:]:
        copy.start()

    barrier = pltpu.get_barrier_semaphore()
    pl.semaphore_signal(barrier, inc=1, device_id=(y * 2 + other, me), device_id_type=MESH)
    for d in range(1, layers):
        yy = lax.rem(y + d, layers)
        pl.semaphore_signal(barrier, inc=1, device_id=(yy * 2 + core, me), device_id_type=MESH)
    for d in range(1, owners):
        pl.semaphore_signal(
            barrier, inc=1, device_id=(g, lax.rem(me + d, owners)), device_id_type=MESH
        )

    small[0].wait()
    cpad[...] = jnp.zeros_like(cpad)
    cpad[:, :nact] = cv[...]
    c32[...] = jnp.zeros_like(c32)
    c32[:nbasis, :] = cpad[...].astype(F32)
    span = -(-slab // 256) * 256
    slab_t = c32[pl.ds(g * slab, span), :].T[:nact].astype(BF16)

    def quarter_step(k, carry):
        x_copy(k).wait()
        where = pl.ds(pl.multiple_of(k * chunk, 16), chunk)
        qv[where, :] = jnp.dot(xv[where, :], cpad[...], preferred_element_type=F32)
        return carry

    def half_part(first, count, fresh):
        for i in range(rows_dev):
            q = qv[pl.ds(first * rows_dev + i, count, stride=rows_dev), :].astype(BF16)
            part = jnp.dot(slab_t[:, first : first + count], q, preferred_element_type=F32)
            spot = pl.ds(i, nact, stride=rows_dev)
            pv[spot, :] = part if fresh else pv[spot, :] + part

    lax.fori_loop(0, early, quarter_step, 0)
    cut = early * chunk // rows_dev // 256 * 256
    if cut:
        half_part(0, cut, True)
    lax.fori_loop(early, nchunks, quarter_step, 0)
    half_part(cut, slab - cut, not cut)

    pl.semaphore_wait(barrier, layers + owners - 1)

    steps = owners // 2
    srows = 2 * orows

    def spot_of(step):
        b = lax.rem(me // 2 + steps // 2 + step, steps)
        return b, pl.multiple_of(b * srows, 8)

    def core_copy(d, step):
        layer = lax.rem(y + d, layers)
        _, at = spot_of(step)
        src = pl.multiple_of((layer * 2 + other) * grows + at, 8)
        return pltpu.make_async_remote_copy(
            src_ref=pv.at[pl.ds(src, srows), :],
            dst_ref=from_core.at[d, pl.ds(at, srows), :],
            send_sem=core_send.at[d, step],
            recv_sem=core_recv.at[d, step],
            device_id=(y * 2 + other, me),
            device_id_type=MESH,
        )

    def y_copy(d, step):
        layer = lax.rem(y + d, layers)
        _, at = spot_of(step)
        return pltpu.make_async_remote_copy(
            src_ref=kept.at[d, pl.ds(at, srows), :],
            dst_ref=from_y.at[d - 1, pl.ds(at, srows), :],
            send_sem=y_send.at[d - 1, step],
            recv_sem=y_recv.at[d - 1, step],
            device_id=(layer * 2 + core, me),
            device_id_type=MESH,
        )

    def pair_copy(d):
        to = lax.rem(me + d, owners)
        return pltpu.make_async_remote_copy(
            src_ref=summed.at[pl.ds(pl.multiple_of(to * orows, 8), orows), :],
            dst_ref=flat.at[pl.ds(pl.multiple_of(me * orows, 8), orows), :],
            send_sem=pair_send.at[d],
            recv_sem=pair_recv.at[d],
            device_id=(g, to),
            device_id_type=MESH,
        )

    order = list(range(1, layers)) + [0]
    for d in order:
        for step in range(steps):
            core_copy(d, step).start()
    for d in order:
        for step in range(steps):
            core_copy(d, step).wait_recv()
            _, at = spot_of(step)
            layer = lax.rem(y + d, layers)
            src = pl.multiple_of((layer * 2 + core) * grows + at, 8)
            here = pl.ds(at, srows)
            kept[d, here, :] = pv[pl.ds(src, srows), :] + from_core[d, here, :]
            if d:
                y_copy(d, step).start()

    for copy in small[1:]:
        copy.wait()
    cols = nsecond * nact
    mu_col = as_column(muv[...].astype(F32), all_rows)
    nu_col = as_column(nuv[...].astype(F32), all_rows)
    basis = lax.broadcasted_iota(jnp.int32, (all_rows, nbasis), 1).astype(F32)
    pick = jnp.where(basis == mu_col, 1.0, 0.0).astype(BF16)
    picked = jnp.dot(pick, cv[...], preferred_element_type=F32).astype(BF16)
    section = section_of((nact, cols), nact, nsecond)
    inside = lax.broadcasted_iota(jnp.int32, (nact, cols), 1) - section * nact
    spread = jnp.where(
        inside == lax.broadcasted_iota(jnp.int32, (nact, cols), 0), 1.0, 0.0
    ).astype(BF16)
    wide = jnp.dot(picked, spread, preferred_element_type=F32)
    nu_of_col = section_of((all_rows, cols), nact, nsecond).astype(F32)
    amat_ref[...] = jnp.where(nu_of_col == nu_col, wide, 0.0).astype(BF16)
    act_row = actv[...].astype(F32)
    act_wide = jnp.dot(
        jnp.broadcast_to(act_row, (8, nact)).astype(BF16), spread, preferred_element_type=F32
    )
    sec8 = section_of((8, cols), nact, nsecond)
    ao_sel = jnp.where(
        lax.broadcasted_iota(jnp.int32, (nsecond, cols), 0)
        == section_of((nsecond, cols), nact, nsecond),
        1.0,
        0.0,
    ).astype(BF16)
    ao_wide = jnp.dot(
        jnp.broadcast_to(aov[...].astype(F32), (8, nsecond)).astype(BF16),
        ao_sel,
        preferred_element_type=F32,
    )
    del sec8
    right_ref[...] = jnp.bitwise_xor(act_wide.astype(jnp.int32), ao_wide.astype(jnp.int32))
    actcol_ref[...] = jnp.broadcast_to(as_column(act_row, nact), (nact, LANES)).astype(jnp.int32)

    for step in range(steps):
        b, at = spot_of(step)
        here = pl.ds(at, srows)
        total = kept[0, here, :]
        for d in range(1, layers):
            y_copy(d, step).wait_recv()
            total = total + from_y[d - 1, here, :]
        summed[here, :] = total
        for half in range(2):
            to = b * 2 + half

            @pl.when(to != me)
            def _():
                gap = lax.rem(to - me + owners, owners)
                pair_copy(gap).start()

    own = pl.ds(pl.multiple_of(me * orows, 8), orows)
    flat[own, :] = summed[own, :]
    for d in range(1, owners):
        pair_copy(d).wait_recv()
    flat_ref[...] = flat[...]
    for d in order:
        for step in range(steps):
            core_copy(d, step).wait_send()
            if d:
                y_copy(d, step).wait_send()
    for d in range(1, owners):
        pair_copy(d).wait_send()


def finish_kernel(dims, act_ref, flat_ref, amat_ref, right_ref, actcol_ref, out_ref):
    owners, rows_dev, per_owner, nact, cols = dims
    block = lax.axis_index("grp") * owners + lax.axis_index("pair")
    a = amat_ref[...]
    weights = jnp.concatenate([a, a, a], axis=0)
    right = right_ref[:1, :]
    act_col = actcol_ref[:, :1]
    for j in range(per_owner):
        f = jnp.concatenate(
            [
                flat_ref[pl.ds((s * per_owner + j) * rows_dev, rows_dev), :]
                for s in range(owners)
            ],
            axis=0,
        )
        high = f.astype(BF16)
        rest = f - high.astype(F32)
        mid = rest.astype(BF16)
        low = (rest - mid.astype(F32)).astype(BF16)
        parts = jnp.concatenate([high, mid, low], axis=0).astype(F32).T[:nact].astype(BF16)
        full = jnp.dot(parts, weights, preferred_element_type=F32)
        left = jnp.bitwise_xor(act_col, act_ref[block * per_owner + j])
        out_ref[pl.ds(j * nact, nact), :] = jnp.where(left == right, full, 0.0)


def fast(integrals, coeff, mu_index, nu_index, ao_irrep, act_irrep):
    rows_dev, slab, nbasis = integrals.shape
    nact = coeff.shape[1]
    groups, owners = lax.axis_size("grp"), lax.axis_size("pair")
    all_rows, nsecond = mu_index.shape[0], ao_irrep.shape[0]
    layers = groups // 2
    per_owner = nact // groups // owners
    grows = nact // groups * rows_dev
    cols = nsecond * nact
    rows = slab * rows_dev
    chunk = max(c for c in range(16, 513, 16) if rows % c == 0)
    nchunks = rows // chunk
    early = min(nchunks, -(-256 * rows_dev // chunk))
    dims = (groups, owners, slab, rows_dev, nbasis, nact, nsecond, all_rows, chunk, early)
    span = -(-slab // 256) * 256
    x = integrals.transpose(1, 0, 2).reshape(rows, nbasis)
    steps = owners // 2
    any_spec = pl.BlockSpec(memory_space=pl.ANY)
    vmem = pl.BlockSpec(memory_space=pltpu.VMEM)
    flat, amat, right, actcol = pl.pallas_call(
        functools.partial(transform_kernel, dims),
        out_shape=(
            jax.ShapeDtypeStruct((grows, LANES), F32),
            jax.ShapeDtypeStruct((all_rows, cols), BF16),
            jax.ShapeDtypeStruct((8, cols), jnp.int32),
            jax.ShapeDtypeStruct((nact, LANES), jnp.int32),
        ),
        in_specs=[any_spec] * 6,
        out_specs=(vmem,) * 4,
        scratch_shapes=[
            pltpu.VMEM((rows, nbasis), BF16),
            pltpu.VMEM((nbasis, nact), BF16),
            pltpu.VMEM((nbasis, LANES), BF16),
            pltpu.VMEM((slab * (groups - 1) + span + 8, LANES), F32),
            pltpu.VMEM((rows, LANES), F32),
            pltpu.VMEM((nact * rows_dev, LANES), F32),
            pltpu.VMEM((1, all_rows), jnp.int32),
            pltpu.VMEM((1, all_rows), jnp.int32),
            pltpu.VMEM((1, nsecond), jnp.int32),
            pltpu.VMEM((1, nact), jnp.int32),
            pltpu.VMEM((layers, grows, LANES), F32),
            pltpu.VMEM((layers, grows, LANES), F32),
            pltpu.VMEM((layers - 1, grows, LANES), F32),
            pltpu.VMEM((grows, LANES), F32),
            pltpu.VMEM((grows, LANES), F32),
            pltpu.SemaphoreType.DMA((nchunks,)),
            pltpu.SemaphoreType.DMA((5,)),
            pltpu.SemaphoreType.DMA((layers, steps)),
            pltpu.SemaphoreType.DMA((layers, steps)),
            pltpu.SemaphoreType.DMA((layers - 1, steps)),
            pltpu.SemaphoreType.DMA((layers - 1, steps)),
            pltpu.SemaphoreType.DMA((owners,)),
            pltpu.SemaphoreType.DMA((owners,)),
        ],
        compiler_params=pltpu.CompilerParams(
            collective_id=0, has_side_effects=True, vmem_limit_bytes=48 * 1024 * 1024
        ),
        cost_estimate=pl.CostEstimate(
            flops=2 * rows * nbasis * nact, bytes_accessed=rows * nbasis * 2, transcendentals=0
        ),
    )(
        x, coeff, mu_index.reshape(1, -1), nu_index.reshape(1, -1),
        ao_irrep.reshape(1, -1), act_irrep.reshape(1, -1),
    )
    return pl.pallas_call(
        functools.partial(finish_kernel, (owners, rows_dev, per_owner, nact, cols)),
        out_shape=jax.ShapeDtypeStruct((per_owner * nact, cols), F32),
        in_specs=[pl.BlockSpec(memory_space=pltpu.SMEM)] + [vmem] * 4,
        out_specs=vmem,
        compiler_params=pltpu.CompilerParams(vmem_limit_bytes=32 * 1024 * 1024),
    )(act_irrep, flat, amat, right, actcol)


def on_device(integrals, coeff, mu_index, nu_index, ao_irrep, act_irrep):
    rows_dev, slab, _ = integrals.shape
    nact = coeff.shape[1]
    groups, owners = lax.axis_size("grp"), lax.axis_size("pair")
    whole_rows = nact % (groups * owners) == 0
    fits = rows_dev == 8 and groups % 2 == 0 and groups > 2 and owners % 2 == 0
    if whole_rows and fits and slab * rows_dev % 16 == 0 and nact <= LANES:
        return fast(integrals, coeff, mu_index, nu_index, ao_irrep, act_irrep)
    return generic(integrals, coeff, mu_index, nu_index, ao_irrep, act_irrep)


def solution(mesh):
    in_specs = (P("pair", "grp", None), P(), P(), P(), P(), P())
    out_specs = P(("grp", "pair"), None)
    return jax.shard_map(
        on_device, mesh=mesh, in_specs=in_specs, out_specs=out_specs, check_vma=False
    )
```

```python
import functools

import jax
import jax.numpy as jnp
from jax import lax
from jax.experimental import pallas as pl
from jax.experimental.pallas import tpu as pltpu
from jax.sharding import PartitionSpec as P

MESH = pl.DeviceIdType.MESH
F32 = jnp.float32
BF16 = jnp.bfloat16
LANES = 128
VMEM_LIMIT = 64 * 1024 * 1024


def generic(integrals, coeff, mu_index, nu_index, ao_irrep, act_irrep):
    rows_dev, slab, nbasis = integrals.shape
    nactive = coeff.shape[1]
    groups = lax.axis_size("grp")
    owners = lax.axis_size("pair")
    total = nactive * nactive
    share = total // groups
    subset = share // owners
    all_rows = mu_index.shape[0]
    nsecond = ao_irrep.shape[0]
    slab_coeff = lax.dynamic_slice_in_dim(coeff, lax.axis_index("grp") * slab, slab, 0)
    rows_first = integrals.transpose(1, 0, 2).reshape(slab * rows_dev, nbasis)
    quarter = jnp.dot(rows_first, coeff, preferred_element_type=F32)
    quarter = quarter.astype(BF16).reshape(slab, rows_dev, nactive)
    partial_value = jnp.einsum("lp,lrq->rpq", slab_coeff, quarter, preferred_element_type=F32)
    partial_value = partial_value.reshape(rows_dev, total)
    mine = lax.psum_scatter(partial_value, "grp", scatter_dimension=1, tiled=True)
    picked = jnp.take(coeff, mu_index, axis=0).astype(F32)
    onehot = (nu_index[:, None] == jnp.arange(nsecond, dtype=jnp.int32)[None, :]).astype(F32)
    amat = (onehot[:, :, None] * picked[:, None, :]).reshape(all_rows, nsecond * nactive)
    sectioned = mine.reshape(rows_dev, owners, subset)
    arrived = lax.all_to_all(sectioned, "pair", split_axis=1, concat_axis=0, tiled=True)
    flat = arrived.reshape(all_rows, arrived.shape[2])
    full = lax.dot_general(flat, amat, (((0,), (0,)), ((), ())), precision=lax.Precision.HIGHEST)
    block_id = lax.axis_index("grp") * owners + lax.axis_index("pair")
    pair_ids = block_id * subset + jnp.arange(subset, dtype=jnp.int32)
    left_irrep = jnp.bitwise_xor(
        jnp.take(act_irrep, pair_ids // nactive), jnp.take(act_irrep, pair_ids % nactive)
    )
    col_ids = jnp.arange(nsecond * nactive, dtype=jnp.int32)
    right_irrep = jnp.bitwise_xor(
        jnp.take(ao_irrep, col_ids // nactive), jnp.take(act_irrep, col_ids % nactive)
    )
    allowed = left_irrep[:, None] == right_irrep[None, :]
    return jnp.where(allowed, full, jnp.zeros_like(full))


def section_of(shape, nactive, nsecond):
    col = lax.broadcasted_iota(jnp.int32, shape, 1)
    section = jnp.zeros(shape, jnp.int32)
    for n in range(1, nsecond):
        section = section + jnp.where(col >= n * nactive, 1, 0)
    return section


def transform_kernel(
    dims, x_hbm, c_hbm, mu_hbm, nu_hbm, ao_hbm, act_hbm, out_hbm,
    xv, cv, ct, cpad, c32, qv, pv, muv, nuv, aov, actv, from_core, kept, from_y, summed, flat,
    picked, nu_col, act_col, out, out_sem, x_sem, in_sem, core_send, core_recv, y_send, y_recv, pair_send, pair_recv,
):
    groups, owners, slab, rows_dev, nbasis, nact, nsecond, all_rows, chunk, early = dims
    layers = groups // 2
    per_group = nact // groups
    per_owner = per_group // owners
    grows = per_group * rows_dev
    orows = per_owner * rows_dev
    g = lax.axis_index("grp")
    me = lax.axis_index("pair")
    y, core = g // 2, g % 2
    other = 1 - core
    nchunks = slab * rows_dev // chunk

    small = [
        pltpu.make_async_copy(src, dst, in_sem.at[k])
        for k, (src, dst) in enumerate(
            ((c_hbm, cv), (mu_hbm, muv), (nu_hbm, nuv), (ao_hbm, aov), (act_hbm, actv))
        )
    ]
    small[0].start()

    def x_copy(k):
        where = pl.ds(pl.multiple_of(k * chunk, 16), chunk)
        return pltpu.make_async_copy(x_hbm.at[where, :], xv.at[where, :], x_sem.at[k])

    for k in range(nchunks):
        x_copy(k).start()
    for copy in small[1:]:
        copy.start()

    barrier = pltpu.get_barrier_semaphore()
    pl.semaphore_signal(barrier, inc=1, device_id=(y * 2 + other, me), device_id_type=MESH)
    for d in range(1, layers):
        yy = lax.rem(y + d, layers)
        pl.semaphore_signal(barrier, inc=1, device_id=(yy * 2 + core, me), device_id_type=MESH)
    for d in range(1, owners):
        pl.semaphore_signal(
            barrier, inc=1, device_id=(g, lax.rem(me + d, owners)), device_id_type=MESH
        )

    small[0].wait()
    ct[...] = jnp.zeros_like(ct)
    ct[:nact, :nbasis] = cv[...].astype(F32)
    c32[...] = ct[...].T
    cpad[...] = c32[:nbasis, :].astype(BF16)

    def quarter_step(k, carry):
        x_copy(k).wait()
        where = pl.ds(pl.multiple_of(k * chunk, 16), chunk)
        qv[where, :] = jnp.dot(xv[where, :], cpad[...], preferred_element_type=F32)
        return carry

    def half_part(first, count, fresh):
        for i in range(0, rows_dev, 2):
            q = jnp.concatenate(
                [
                    qv[pl.ds(first * rows_dev + i + k, count, stride=rows_dev), :].astype(BF16)
                    for k in range(2)
                ],
                axis=1,
            )
            part = jnp.dot(slab_t[:, first : first + count], q, preferred_element_type=F32)
            for k in range(2):
                spot = pl.ds(i + k, nact, stride=rows_dev)
                mine = part[:, k * LANES : (k + 1) * LANES]
                pv[spot, :] = mine if fresh else pv[spot, :] + mine

    lax.fori_loop(0, early, quarter_step, 0)
    span = -(-slab // 256) * 256
    slab_t = c32[pl.ds(g * slab, span), :].T[:nact].astype(BF16)
    cut = early * chunk // rows_dev // 256 * 256
    if cut:
        half_part(0, cut, True)
    lax.fori_loop(early, nchunks, quarter_step, 0)
    half_part(cut, slab - cut, not cut)

    pl.semaphore_wait(barrier, layers + owners - 1)

    steps = owners // 2
    srows = 2 * orows

    def spot_of(step):
        b = lax.rem(me // 2 + steps // 2 + step, steps)
        return b, pl.multiple_of(b * srows, 8)

    def core_copy(d, step):
        layer = lax.rem(y + d, layers)
        _, at = spot_of(step)
        src = pl.multiple_of((layer * 2 + other) * grows + at, 8)
        return pltpu.make_async_remote_copy(
            src_ref=pv.at[pl.ds(src, srows), :],
            dst_ref=from_core.at[d, pl.ds(at, srows), :],
            send_sem=core_send.at[d, step],
            recv_sem=core_recv.at[d, step],
            device_id=(y * 2 + other, me),
            device_id_type=MESH,
        )

    def y_copy(d, step):
        layer = lax.rem(y + d, layers)
        _, at = spot_of(step)
        return pltpu.make_async_remote_copy(
            src_ref=kept.at[d, pl.ds(at, srows), :],
            dst_ref=from_y.at[d - 1, pl.ds(at, srows), :],
            send_sem=y_send.at[d - 1, step],
            recv_sem=y_recv.at[d - 1, step],
            device_id=(layer * 2 + core, me),
            device_id_type=MESH,
        )

    def pair_copy(d):
        to = lax.rem(me + d, owners)
        return pltpu.make_async_remote_copy(
            src_ref=summed.at[pl.ds(pl.multiple_of(to * orows, 8), orows), :],
            dst_ref=flat.at[pl.ds(pl.multiple_of(me * orows, 8), orows), :],
            send_sem=pair_send.at[d],
            recv_sem=pair_recv.at[d],
            device_id=(g, to),
            device_id_type=MESH,
        )

    order = list(range(1, layers)) + [0]
    for d in order:
        for step in range(steps):
            core_copy(d, step).start()
    for d in order:
        for step in range(steps):
            core_copy(d, step).wait_recv()
            _, at = spot_of(step)
            layer = lax.rem(y + d, layers)
            src = pl.multiple_of((layer * 2 + core) * grows + at, 8)
            here = pl.ds(at, srows)
            kept[d, here, :] = pv[pl.ds(src, srows), :] + from_core[d, here, :]
            if d:
                y_copy(d, step).start()

    for step in range(steps):
        b, at = spot_of(step)
        here = pl.ds(at, srows)
        total = kept[0, here, :]
        for d in range(1, layers):
            y_copy(d, step).wait_recv()
            total = total + from_y[d - 1, here, :]
        summed[here, :] = total
        for half in range(2):
            to = b * 2 + half

            @pl.when(to != me)
            def _():
                gap = lax.rem(to - me + owners, owners)
                pair_copy(gap).start()

    own = pl.ds(pl.multiple_of(me * orows, 8), orows)
    flat[own, :] = summed[own, :]
    for copy in small[1:]:
        copy.wait()
    cols = nsecond * nact

    def pick_row(i, carry):
        picked[pl.ds(i, 1), :] = c32[pl.ds(muv[i], 1), :]
        nu_col[pl.ds(i, 1), :] = jnp.broadcast_to(nuv[i], (1, LANES))
        return carry

    def act_row(i, carry):
        act_col[pl.ds(i, 1), :] = jnp.broadcast_to(actv[i], (1, LANES))
        return carry

    lax.fori_loop(0, all_rows, pick_row, 0)
    lax.fori_loop(0, nact, act_row, 0)
    section = section_of((1, cols), nact, nsecond)
    inside = lax.broadcasted_iota(jnp.int32, (1, cols), 1) - section * nact
    spread = inside == lax.broadcasted_iota(jnp.int32, (nact, cols), 0)
    wide = jnp.dot(
        picked[:, :nact].astype(BF16),
        jnp.where(spread, 1.0, 0.0).astype(BF16),
        preferred_element_type=F32,
    )
    amat = jnp.where(section == nu_col[:, :1], wide, 0.0).astype(BF16)
    weights = jnp.concatenate([amat, amat, amat], axis=0)
    act_wide = jnp.sum(
        jnp.where(spread, act_col[:, :1].astype(F32), 0.0), axis=0, keepdims=True
    ).astype(jnp.int32)
    ao_wide = jnp.zeros((1, cols), jnp.int32)
    for n in range(nsecond):
        ao_wide = jnp.where(section == n, aov[n], ao_wide)
    right = jnp.bitwise_xor(act_wide, ao_wide)

    for d in range(1, owners):
        pair_copy(d).wait_recv()
    copies = []
    for j in range(per_owner):
        f = jnp.concatenate(
            [
                flat[pl.ds((s * per_owner + j) * rows_dev, rows_dev), :]
                for s in range(owners)
            ],
            axis=0,
        )
        high = f.astype(BF16)
        rest = f - high.astype(F32)
        mid = rest.astype(BF16)
        low = (rest - mid.astype(F32)).astype(BF16)
        parts = jnp.concatenate([high, mid, low], axis=0).astype(F32).T[:nact].astype(BF16)
        full = jnp.dot(parts, weights, preferred_element_type=F32)
        p = (g * owners + me) * per_owner + j
        left = jnp.bitwise_xor(act_col[:, :1], act_col[pl.ds(p, 1), :1])
        here = pl.ds(j * nact, nact)
        out[here, :] = jnp.where(left == right, full, 0.0)
        copies.append(pltpu.make_async_copy(out.at[here, :], out_hbm.at[here, :], out_sem.at[j]))
        copies[-1].start()
    for d in order:
        for step in range(steps):
            core_copy(d, step).wait_send()
            if d:
                y_copy(d, step).wait_send()
    for d in range(1, owners):
        pair_copy(d).wait_send()
    for copy in copies:
        copy.wait()


def fast(integrals, coeff, mu_index, nu_index, ao_irrep, act_irrep):
    rows_dev, slab, nbasis = integrals.shape
    nact = coeff.shape[1]
    groups, owners = lax.axis_size("grp"), lax.axis_size("pair")
    all_rows, nsecond = mu_index.shape[0], ao_irrep.shape[0]
    layers = groups // 2
    per_owner = nact // groups // owners
    grows = nact // groups * rows_dev
    cols = nsecond * nact
    rows = slab * rows_dev
    chunk = max(c for c in range(16, 513, 16) if rows % c == 0)
    nchunks = rows // chunk
    early = min(nchunks, -(-256 * rows_dev // chunk))
    dims = (groups, owners, slab, rows_dev, nbasis, nact, nsecond, all_rows, chunk, early)
    span = -(-slab // 256) * 256
    deep = -(-(slab * (groups - 1) + span) // LANES) * LANES
    x = integrals.transpose(1, 0, 2).reshape(rows, nbasis)
    steps = owners // 2
    hbm = pl.BlockSpec(memory_space=pltpu.HBM)
    return pl.pallas_call(
        functools.partial(transform_kernel, dims),
        out_shape=jax.ShapeDtypeStruct((per_owner * nact, cols), F32),
        in_specs=[hbm] * 6,
        out_specs=hbm,
        scratch_shapes=[
            pltpu.VMEM((rows, nbasis), BF16),
            pltpu.VMEM((nact, nbasis), BF16),
            pltpu.VMEM((LANES, deep), F32),
            pltpu.VMEM((nbasis, LANES), BF16),
            pltpu.VMEM((deep, LANES), F32),
            pltpu.VMEM((rows, LANES), F32),
            pltpu.VMEM((nact * rows_dev, LANES), F32),
            pltpu.SMEM((all_rows,), jnp.int32),
            pltpu.SMEM((all_rows,), jnp.int32),
            pltpu.SMEM((nsecond,), jnp.int32),
            pltpu.SMEM((nact,), jnp.int32),
            pltpu.VMEM((layers, grows, LANES), F32),
            pltpu.VMEM((layers, grows, LANES), F32),
            pltpu.VMEM((layers - 1, grows, LANES), F32),
            pltpu.VMEM((grows, LANES), F32),
            pltpu.VMEM((grows, LANES), F32),
            pltpu.VMEM((all_rows, LANES), F32),
            pltpu.VMEM((all_rows, LANES), jnp.int32),
            pltpu.VMEM((nact, LANES), jnp.int32),
            pltpu.VMEM((per_owner * nact, cols), F32),
            pltpu.SemaphoreType.DMA((per_owner,)),
            pltpu.SemaphoreType.DMA((nchunks,)),
            pltpu.SemaphoreType.DMA((5,)),
            pltpu.SemaphoreType.DMA((layers, steps)),
            pltpu.SemaphoreType.DMA((layers, steps)),
            pltpu.SemaphoreType.DMA((layers - 1, steps)),
            pltpu.SemaphoreType.DMA((layers - 1, steps)),
            pltpu.SemaphoreType.DMA((owners,)),
            pltpu.SemaphoreType.DMA((owners,)),
        ],
        compiler_params=pltpu.CompilerParams(
            collective_id=0, has_side_effects=True, vmem_limit_bytes=VMEM_LIMIT
        ),
        cost_estimate=pl.CostEstimate(
            flops=2 * rows * nbasis * nact, bytes_accessed=rows * nbasis * 2, transcendentals=0
        ),
    )(x, coeff.T, mu_index, nu_index, ao_irrep, act_irrep)


def on_device(integrals, coeff, mu_index, nu_index, ao_irrep, act_irrep):
    rows_dev, slab, _ = integrals.shape
    nact = coeff.shape[1]
    groups, owners = lax.axis_size("grp"), lax.axis_size("pair")
    whole_rows = nact % (groups * owners) == 0
    fits = rows_dev == 8 and groups % 2 == 0 and groups > 2 and owners % 2 == 0
    if whole_rows and fits and slab * rows_dev % 16 == 0 and nact <= LANES:
        return fast(integrals, coeff, mu_index, nu_index, ao_irrep, act_irrep)
    return generic(integrals, coeff, mu_index, nu_index, ao_irrep, act_irrep)


def solution(mesh):
    in_specs = (P("pair", "grp", None), P(), P(), P(), P(), P())
    out_specs = P(("grp", "pair"), None)
    return jax.shard_map(
        on_device, mesh=mesh, in_specs=in_specs, out_specs=out_specs, check_vma=False
    )
```

```python
import functools

import jax
import jax.numpy as jnp
from jax import lax
from jax.experimental import pallas as pl
from jax.experimental.pallas import tpu as pltpu
from jax.sharding import PartitionSpec as P

MESH = pl.DeviceIdType.MESH
F32 = jnp.float32
BF16 = jnp.bfloat16
LANES = 128
VMEM_LIMIT = 64 * 1024 * 1024


def generic(integrals, coeff, mu_index, nu_index, ao_irrep, act_irrep):
    rows_dev, slab, nbasis = integrals.shape
    nactive = coeff.shape[1]
    groups = lax.axis_size("grp")
    owners = lax.axis_size("pair")
    total = nactive * nactive
    share = total // groups
    subset = share // owners
    all_rows = mu_index.shape[0]
    nsecond = ao_irrep.shape[0]
    slab_coeff = lax.dynamic_slice_in_dim(coeff, lax.axis_index("grp") * slab, slab, 0)
    rows_first = integrals.transpose(1, 0, 2).reshape(slab * rows_dev, nbasis)
    quarter = jnp.dot(rows_first, coeff, preferred_element_type=F32)
    quarter = quarter.astype(BF16).reshape(slab, rows_dev, nactive)
    partial_value = jnp.einsum("lp,lrq->rpq", slab_coeff, quarter, preferred_element_type=F32)
    partial_value = partial_value.reshape(rows_dev, total)
    mine = lax.psum_scatter(partial_value, "grp", scatter_dimension=1, tiled=True)
    picked = jnp.take(coeff, mu_index, axis=0).astype(F32)
    onehot = (nu_index[:, None] == jnp.arange(nsecond, dtype=jnp.int32)[None, :]).astype(F32)
    amat = (onehot[:, :, None] * picked[:, None, :]).reshape(all_rows, nsecond * nactive)
    sectioned = mine.reshape(rows_dev, owners, subset)
    arrived = lax.all_to_all(sectioned, "pair", split_axis=1, concat_axis=0, tiled=True)
    flat = arrived.reshape(all_rows, arrived.shape[2])
    full = lax.dot_general(flat, amat, (((0,), (0,)), ((), ())), precision=lax.Precision.HIGHEST)
    block_id = lax.axis_index("grp") * owners + lax.axis_index("pair")
    pair_ids = block_id * subset + jnp.arange(subset, dtype=jnp.int32)
    left_irrep = jnp.bitwise_xor(
        jnp.take(act_irrep, pair_ids // nactive), jnp.take(act_irrep, pair_ids % nactive)
    )
    col_ids = jnp.arange(nsecond * nactive, dtype=jnp.int32)
    right_irrep = jnp.bitwise_xor(
        jnp.take(ao_irrep, col_ids // nactive), jnp.take(act_irrep, col_ids % nactive)
    )
    allowed = left_irrep[:, None] == right_irrep[None, :]
    return jnp.where(allowed, full, jnp.zeros_like(full))


def section_of(shape, nactive, nsecond):
    col = lax.broadcasted_iota(jnp.int32, shape, 1)
    section = jnp.zeros(shape, jnp.int32)
    for n in range(1, nsecond):
        section = section + jnp.where(col >= n * nactive, 1, 0)
    return section


def transform_kernel(
    dims, x_hbm, c_hbm, mu_hbm, nu_hbm, ao_hbm, act_hbm, flat_hbm, amat_hbm, right_hbm, act_out,
    xv, cv, st, ct, c32, qv, pv, muv, nuv, aov, actv, from_core, kept, from_y, summed, flat,
    picked, nu_col, amat_ref, right_ref, act_col, out_sem, x_sem, in_sem, core_send, core_recv, y_send, y_recv, pair_send, pair_recv,
):
    groups, owners, slab, rows_dev, nbasis, nact, nsecond, all_rows, chunk, early = dims
    layers = groups // 2
    per_group = nact // groups
    per_owner = per_group // owners
    grows = per_group * rows_dev
    orows = per_owner * rows_dev
    g = lax.axis_index("grp")
    me = lax.axis_index("pair")
    y, core = g // 2, g % 2
    other = 1 - core
    nchunks = slab * rows_dev // chunk

    small = [
        pltpu.make_async_copy(src, dst, in_sem.at[k])
        for k, (src, dst) in enumerate(
            ((c_hbm, cv.at[pl.ds(0, nact), :]), (mu_hbm, muv), (nu_hbm, nuv), (ao_hbm, aov), (act_hbm, actv))
        )
    ]
    small[0].start()

    def x_copy(k):
        where = pl.ds(pl.multiple_of(k * chunk, 16), chunk)
        return pltpu.make_async_copy(x_hbm.at[where, :], xv.at[where, :], x_sem.at[k])

    for k in range(nchunks):
        x_copy(k).start()
    for copy in small[1:]:
        copy.start()

    barrier = pltpu.get_barrier_semaphore()
    pl.semaphore_signal(barrier, inc=1, device_id=(y * 2 + other, me), device_id_type=MESH)
    for d in range(1, layers):
        yy = lax.rem(y + d, layers)
        pl.semaphore_signal(barrier, inc=1, device_id=(yy * 2 + core, me), device_id_type=MESH)
    for d in range(1, owners):
        pl.semaphore_signal(
            barrier, inc=1, device_id=(g, lax.rem(me + d, owners)), device_id_type=MESH
        )

    cv[nact:, :] = jnp.zeros((LANES - nact, nbasis), BF16)
    small[0].wait()
    for k in range(groups):

        @pl.when(g == k)
        def _():
            st[:, :slab] = cv[:nact, k * slab : (k + 1) * slab]


    def quarter_step(k, carry):
        x_copy(k).wait()
        where = pl.ds(pl.multiple_of(k * chunk, 16), chunk)
        qv[where, :] = lax.dot_general(
            xv[where, :], cv[...], (((1,), (1,)), ((), ())), preferred_element_type=F32
        )
        return carry

    def half_part(first, count, fresh):
        for i in range(0, rows_dev, 2):
            q = jnp.concatenate(
                [
                    qv[pl.ds(first * rows_dev + i + k, count, stride=rows_dev), :].astype(BF16)
                    for k in range(2)
                ],
                axis=1,
            )
            part = jnp.dot(st[:, first : first + count], q, preferred_element_type=F32)
            for k in range(2):
                spot = pl.ds(i + k, nact, stride=rows_dev)
                mine = part[:, k * LANES : (k + 1) * LANES]
                pv[spot, :] = mine if fresh else pv[spot, :] + mine

    lax.fori_loop(0, early, quarter_step, 0)
    cut = early * chunk // rows_dev // 256 * 256
    if cut:
        half_part(0, cut, True)
    lax.fori_loop(early, nchunks, quarter_step, 0)
    half_part(cut, slab - cut, not cut)

    pl.semaphore_wait(barrier, layers + owners - 1)

    steps = owners // 2
    srows = 2 * orows

    def spot_of(step):
        b = lax.rem(me // 2 + steps // 2 + step, steps)
        return b, pl.multiple_of(b * srows, 8)

    def core_copy(d, step):
        layer = lax.rem(y + d, layers)
        _, at = spot_of(step)
        src = pl.multiple_of((layer * 2 + other) * grows + at, 8)
        return pltpu.make_async_remote_copy(
            src_ref=pv.at[pl.ds(src, srows), :],
            dst_ref=from_core.at[d, pl.ds(at, srows), :],
            send_sem=core_send.at[d, step],
            recv_sem=core_recv.at[d, step],
            device_id=(y * 2 + other, me),
            device_id_type=MESH,
        )

    def y_copy(d, step):
        layer = lax.rem(y + d, layers)
        _, at = spot_of(step)
        return pltpu.make_async_remote_copy(
            src_ref=kept.at[d, pl.ds(at, srows), :],
            dst_ref=from_y.at[d - 1, pl.ds(at, srows), :],
            send_sem=y_send.at[d - 1, step],
            recv_sem=y_recv.at[d - 1, step],
            device_id=(layer * 2 + core, me),
            device_id_type=MESH,
        )

    def pair_copy(d):
        to = lax.rem(me + d, owners)
        return pltpu.make_async_remote_copy(
            src_ref=summed.at[pl.ds(pl.multiple_of(to * orows, 8), orows), :],
            dst_ref=flat.at[pl.ds(pl.multiple_of(me * orows, 8), orows), :],
            send_sem=pair_send.at[d],
            recv_sem=pair_recv.at[d],
            device_id=(g, to),
            device_id_type=MESH,
        )

    order = list(range(1, layers)) + [0]
    for d in order:
        for step in range(steps):
            core_copy(d, step).start()
    for d in order:
        for step in range(steps):
            core_copy(d, step).wait_recv()
            _, at = spot_of(step)
            layer = lax.rem(y + d, layers)
            src = pl.multiple_of((layer * 2 + core) * grows + at, 8)
            here = pl.ds(at, srows)
            kept[d, here, :] = pv[pl.ds(src, srows), :] + from_core[d, here, :]
            if d:
                y_copy(d, step).start()

    for step in range(steps):
        b, at = spot_of(step)
        here = pl.ds(at, srows)
        total = kept[0, here, :]
        for d in range(1, layers):
            y_copy(d, step).wait_recv()
            total = total + from_y[d - 1, here, :]
        summed[here, :] = total
        for half in range(2):
            to = b * 2 + half

            @pl.when(to != me)
            def _():
                gap = lax.rem(to - me + owners, owners)
                pair_copy(gap).start()

    own = pl.ds(pl.multiple_of(me * orows, 8), orows)
    flat[own, :] = summed[own, :]
    for copy in small[1:]:
        copy.wait()
    cols = nsecond * nact
    ct[...] = jnp.zeros_like(ct)
    ct[:, :nbasis] = cv[...].astype(F32)
    c32[...] = ct[...].T

    def pick_row(i, carry):
        picked[pl.ds(i, 1), :] = c32[pl.ds(muv[i], 1), :]
        nu_col[pl.ds(i, 1), :] = jnp.broadcast_to(nuv[i], (1, LANES))
        return carry

    def act_row(i, carry):
        act_col[pl.ds(i, 1), :] = jnp.broadcast_to(actv[i], (1, LANES))
        return carry

    lax.fori_loop(0, all_rows, pick_row, 0)
    lax.fori_loop(0, nact, act_row, 0)
    section = section_of((1, cols), nact, nsecond)
    inside = lax.broadcasted_iota(jnp.int32, (1, cols), 1) - section * nact
    spread = inside == lax.broadcasted_iota(jnp.int32, (nact, cols), 0)
    wide = jnp.dot(
        picked[:, :nact].astype(BF16),
        jnp.where(spread, 1.0, 0.0).astype(BF16),
        preferred_element_type=F32,
    )
    amat_ref[...] = jnp.where(section == nu_col[:, :1], wide, 0.0).astype(BF16)
    act_wide = jnp.sum(
        jnp.where(spread, act_col[:, :1].astype(F32), 0.0), axis=0, keepdims=True
    ).astype(jnp.int32)
    ao_wide = jnp.zeros((1, cols), jnp.int32)
    for n in range(nsecond):
        ao_wide = jnp.where(section == n, aov[n], ao_wide)
    right_ref[...] = jnp.broadcast_to(jnp.bitwise_xor(act_wide, ao_wide), (8, cols))
    results = [
        pltpu.make_async_copy(src, dst, out_sem.at[k])
        for k, (src, dst) in enumerate(
            (
                (flat, flat_hbm),
                (amat_ref, amat_hbm),
                (right_ref, right_hbm),
                (act_col, act_out),
            )
        )
    ]
    for copy in results[1:]:
        copy.start()

    for d in range(1, owners):
        pair_copy(d).wait_recv()
    results[0].start()
    for d in order:
        for step in range(steps):
            core_copy(d, step).wait_send()
            if d:
                y_copy(d, step).wait_send()
    for d in range(1, owners):
        pair_copy(d).wait_send()
    for copy in results:
        copy.wait()


def finish_kernel(
    dims, flat_hbm, amat_hbm, right_hbm, act_in, out_hbm,
    flat, amat_ref, right_ref, act_col, out, in_sem, out_sem,
):
    owners, rows_dev, per_owner, nact = dims
    first = (lax.axis_index("grp") * owners + lax.axis_index("pair")) * per_owner
    arrived = [
        pltpu.make_async_copy(src, dst, in_sem.at[k])
        for k, (src, dst) in enumerate(
            (
                (flat_hbm, flat),
                (amat_hbm, amat_ref),
                (right_hbm, right_ref),
                (act_in, act_col),
            )
        )
    ]
    for copy in arrived:
        copy.start()
    for copy in arrived:
        copy.wait()
    weights = jnp.concatenate([amat_ref[...]] * 3, axis=0)
    right = right_ref[:1, :]
    copies = []
    for j in range(per_owner):
        f = jnp.concatenate(
            [
                flat[pl.ds((s * per_owner + j) * rows_dev, rows_dev), :]
                for s in range(owners)
            ],
            axis=0,
        )
        high = f.astype(BF16)
        rest = f - high.astype(F32)
        mid = rest.astype(BF16)
        low = (rest - mid.astype(F32)).astype(BF16)
        parts = jnp.concatenate([high, mid, low], axis=0).astype(F32).T[:nact].astype(BF16)
        full = jnp.dot(parts, weights, preferred_element_type=F32)
        p = first + j
        left = jnp.bitwise_xor(act_col[:, :1], act_col[pl.ds(p, 1), :1])
        here = pl.ds(j * nact, nact)
        out[here, :] = jnp.where(left == right, full, 0.0)
        copies.append(pltpu.make_async_copy(out.at[here, :], out_hbm.at[here, :], out_sem.at[j]))
        copies[-1].start()
    for copy in copies:
        copy.wait()


def fast(integrals, coeff, mu_index, nu_index, ao_irrep, act_irrep):
    rows_dev, slab, nbasis = integrals.shape
    nact = coeff.shape[1]
    groups, owners = lax.axis_size("grp"), lax.axis_size("pair")
    all_rows, nsecond = mu_index.shape[0], ao_irrep.shape[0]
    layers = groups // 2
    per_owner = nact // groups // owners
    grows = nact // groups * rows_dev
    cols = nsecond * nact
    rows = slab * rows_dev
    chunk = max(c for c in range(16, 513, 16) if rows % c == 0)
    nchunks = rows // chunk
    early = min(nchunks, -(-256 * rows_dev // chunk))
    dims = (groups, owners, slab, rows_dev, nbasis, nact, nsecond, all_rows, chunk, early)
    span = -(-slab // 256) * 256
    deep = -(-nbasis // LANES) * LANES
    x = integrals.transpose(1, 0, 2).reshape(rows, nbasis)
    steps = owners // 2
    hbm = pl.BlockSpec(memory_space=pltpu.HBM)
    tables = pl.pallas_call(
        functools.partial(transform_kernel, dims),
        out_shape=(
            jax.ShapeDtypeStruct((grows, LANES), F32),
            jax.ShapeDtypeStruct((all_rows, cols), BF16),
            jax.ShapeDtypeStruct((8, cols), jnp.int32),
            jax.ShapeDtypeStruct((nact, LANES), jnp.int32),
        ),
        in_specs=[hbm] * 6,
        out_specs=(hbm,) * 4,
        scratch_shapes=[
            pltpu.VMEM((rows, nbasis), BF16),
            pltpu.VMEM((LANES, nbasis), BF16),
            pltpu.VMEM((nact, span), BF16),
            pltpu.VMEM((LANES, deep), F32),
            pltpu.VMEM((deep, LANES), F32),
            pltpu.VMEM((rows, LANES), F32),
            pltpu.VMEM((nact * rows_dev, LANES), F32),
            pltpu.SMEM((all_rows,), jnp.int32),
            pltpu.SMEM((all_rows,), jnp.int32),
            pltpu.SMEM((nsecond,), jnp.int32),
            pltpu.SMEM((nact,), jnp.int32),
            pltpu.VMEM((layers, grows, LANES), F32),
            pltpu.VMEM((layers, grows, LANES), F32),
            pltpu.VMEM((layers - 1, grows, LANES), F32),
            pltpu.VMEM((grows, LANES), F32),
            pltpu.VMEM((grows, LANES), F32),
            pltpu.VMEM((all_rows, LANES), F32),
            pltpu.VMEM((all_rows, LANES), jnp.int32),
            pltpu.VMEM((all_rows, cols), BF16),
            pltpu.VMEM((8, cols), jnp.int32),
            pltpu.VMEM((nact, LANES), jnp.int32),
            pltpu.SemaphoreType.DMA((4,)),
            pltpu.SemaphoreType.DMA((nchunks,)),
            pltpu.SemaphoreType.DMA((5,)),
            pltpu.SemaphoreType.DMA((layers, steps)),
            pltpu.SemaphoreType.DMA((layers, steps)),
            pltpu.SemaphoreType.DMA((layers - 1, steps)),
            pltpu.SemaphoreType.DMA((layers - 1, steps)),
            pltpu.SemaphoreType.DMA((owners,)),
            pltpu.SemaphoreType.DMA((owners,)),
        ],
        compiler_params=pltpu.CompilerParams(
            collective_id=0, has_side_effects=True, vmem_limit_bytes=VMEM_LIMIT
        ),
        cost_estimate=pl.CostEstimate(
            flops=2 * rows * nbasis * nact, bytes_accessed=rows * nbasis * 2, transcendentals=0
        ),
    )(x, coeff.T, mu_index, nu_index, ao_irrep, act_irrep)
    return pl.pallas_call(
        functools.partial(finish_kernel, (owners, rows_dev, per_owner, nact)),
        out_shape=jax.ShapeDtypeStruct((per_owner * nact, cols), F32),
        in_specs=[hbm] * 4,
        out_specs=hbm,
        scratch_shapes=[
            pltpu.VMEM((grows, LANES), F32),
            pltpu.VMEM((all_rows, cols), BF16),
            pltpu.VMEM((8, cols), jnp.int32),
            pltpu.VMEM((nact, LANES), jnp.int32),
            pltpu.VMEM((per_owner * nact, cols), F32),
            pltpu.SemaphoreType.DMA((4,)),
            pltpu.SemaphoreType.DMA((per_owner,)),
        ],
        compiler_params=pltpu.CompilerParams(vmem_limit_bytes=VMEM_LIMIT),
    )(*tables)


def on_device(integrals, coeff, mu_index, nu_index, ao_irrep, act_irrep):
    rows_dev, slab, _ = integrals.shape
    nact = coeff.shape[1]
    groups, owners = lax.axis_size("grp"), lax.axis_size("pair")
    whole_rows = nact % (groups * owners) == 0
    fits = rows_dev == 8 and groups % 2 == 0 and groups > 2 and owners % 2 == 0
    if whole_rows and fits and slab * rows_dev % 16 == 0 and nact <= LANES:
        return fast(integrals, coeff, mu_index, nu_index, ao_irrep, act_irrep)
    return generic(integrals, coeff, mu_index, nu_index, ao_irrep, act_irrep)


def solution(mesh):
    in_specs = (P("pair", "grp", None), P(), P(), P(), P(), P())
    out_specs = P(("grp", "pair"), None)
    return jax.shard_map(
        on_device, mesh=mesh, in_specs=in_specs, out_specs=out_specs, check_vma=False
    )
```

```python
import functools

import jax
import jax.numpy as jnp
from jax import lax
from jax.experimental import pallas as pl
from jax.experimental.pallas import tpu as pltpu
from jax.sharding import PartitionSpec as P

MESH = pl.DeviceIdType.MESH
F32 = jnp.float32
BF16 = jnp.bfloat16
LANES = 128
VMEM_LIMIT = 64 * 1024 * 1024


def generic(integrals, coeff, mu_index, nu_index, ao_irrep, act_irrep):
    rows_dev, slab, nbasis = integrals.shape
    nactive = coeff.shape[1]
    groups = lax.axis_size("grp")
    owners = lax.axis_size("pair")
    total = nactive * nactive
    share = total // groups
    subset = share // owners
    all_rows = mu_index.shape[0]
    nsecond = ao_irrep.shape[0]
    slab_coeff = lax.dynamic_slice_in_dim(coeff, lax.axis_index("grp") * slab, slab, 0)
    rows_first = integrals.transpose(1, 0, 2).reshape(slab * rows_dev, nbasis)
    quarter = jnp.dot(rows_first, coeff, preferred_element_type=F32)
    quarter = quarter.astype(BF16).reshape(slab, rows_dev, nactive)
    partial_value = jnp.einsum("lp,lrq->rpq", slab_coeff, quarter, preferred_element_type=F32)
    partial_value = partial_value.reshape(rows_dev, total)
    mine = lax.psum_scatter(partial_value, "grp", scatter_dimension=1, tiled=True)
    picked = jnp.take(coeff, mu_index, axis=0).astype(F32)
    onehot = (nu_index[:, None] == jnp.arange(nsecond, dtype=jnp.int32)[None, :]).astype(F32)
    amat = (onehot[:, :, None] * picked[:, None, :]).reshape(all_rows, nsecond * nactive)
    sectioned = mine.reshape(rows_dev, owners, subset)
    arrived = lax.all_to_all(sectioned, "pair", split_axis=1, concat_axis=0, tiled=True)
    flat = arrived.reshape(all_rows, arrived.shape[2])
    full = lax.dot_general(flat, amat, (((0,), (0,)), ((), ())), precision=lax.Precision.HIGHEST)
    block_id = lax.axis_index("grp") * owners + lax.axis_index("pair")
    pair_ids = block_id * subset + jnp.arange(subset, dtype=jnp.int32)
    left_irrep = jnp.bitwise_xor(
        jnp.take(act_irrep, pair_ids // nactive), jnp.take(act_irrep, pair_ids % nactive)
    )
    col_ids = jnp.arange(nsecond * nactive, dtype=jnp.int32)
    right_irrep = jnp.bitwise_xor(
        jnp.take(ao_irrep, col_ids // nactive), jnp.take(act_irrep, col_ids % nactive)
    )
    allowed = left_irrep[:, None] == right_irrep[None, :]
    return jnp.where(allowed, full, jnp.zeros_like(full))


def section_of(shape, nactive, nsecond):
    col = lax.broadcasted_iota(jnp.int32, shape, 1)
    section = jnp.zeros(shape, jnp.int32)
    for n in range(1, nsecond):
        section = section + jnp.where(col >= n * nactive, 1, 0)
    return section


def transform_kernel(
    dims, x_hbm, c_hbm, mu_hbm, nu_hbm, ao_hbm, act_hbm, flat_hbm, amat_hbm, right_hbm, act_out,
    xv, cv, st, cpad, c32, qv, pv, muv, nuv, aov, actv, from_core, kept, from_y, summed, flat,
    picked, nu_col, amat_ref, right_ref, act_col, out_sem, x_sem, in_sem, core_send, core_recv, y_send, y_recv, pair_send, pair_recv,
):
    groups, owners, slab, rows_dev, nbasis, nact, nsecond, all_rows, chunks = dims
    layers = groups // 2
    per_group = nact // groups
    per_owner = per_group // owners
    grows = per_group * rows_dev
    orows = per_owner * rows_dev
    g = lax.axis_index("grp")
    me = lax.axis_index("pair")
    y, core = g // 2, g % 2
    other = 1 - core

    small = [
        pltpu.make_async_copy(src, dst, in_sem.at[k])
        for k, (src, dst) in enumerate(
            ((c_hbm, cv.at[pl.ds(0, nact), :]), (mu_hbm, muv), (nu_hbm, nuv), (ao_hbm, aov), (act_hbm, actv))
        )
    ]
    small[0].start()

    def x_copy(k):
        where = pl.ds(*chunks[k])
        return pltpu.make_async_copy(x_hbm.at[where, :], xv.at[where, :], x_sem.at[k])

    for k in range(len(chunks)):
        x_copy(k).start()
    for copy in small[1:]:
        copy.start()

    barrier = pltpu.get_barrier_semaphore()
    pl.semaphore_signal(barrier, inc=1, device_id=(y * 2 + other, me), device_id_type=MESH)
    for d in range(1, layers):
        yy = lax.rem(y + d, layers)
        pl.semaphore_signal(barrier, inc=1, device_id=(yy * 2 + core, me), device_id_type=MESH)
    for d in range(1, owners):
        pl.semaphore_signal(
            barrier, inc=1, device_id=(g, lax.rem(me + d, owners)), device_id_type=MESH
        )

    cv[nact:, :] = jnp.zeros((LANES - nact, nbasis), BF16)
    small[0].wait()
    cpad[...] = cv[...].T


    def quarter_step(k):
        x_copy(k).wait()
        where = pl.ds(*chunks[k])
        qv[where, :] = jnp.dot(xv[where, :], cpad[...], preferred_element_type=F32)

    def half_part(first, count, fresh):
        for i in range(0, rows_dev, 2):
            q = jnp.concatenate(
                [
                    qv[pl.ds(first * rows_dev + i + k, count, stride=rows_dev), :].astype(BF16)
                    for k in range(2)
                ],
                axis=1,
            )
            part = jnp.dot(st[:, first : first + count], q, preferred_element_type=F32)
            for k in range(2):
                spot = pl.ds(i + k, nact, stride=rows_dev)
                mine = part[:, k * LANES : (k + 1) * LANES]
                pv[spot, :] = mine if fresh else pv[spot, :] + mine

    cut = 0
    for k in range(len(chunks)):
        quarter_step(k)
        if k == 0:
            for part in range(groups):

                @pl.when(g == part)
                def _():
                    st[:, :slab] = cv[:nact, part * slab : (part + 1) * slab]

        if k + 2 == len(chunks) - 1:
            cut = sum(chunks[k]) // rows_dev // 256 * 256
            if cut:
                half_part(0, cut, True)
    half_part(cut, slab - cut, not cut)

    pl.semaphore_wait(barrier, layers + owners - 1)

    steps = owners // 2
    srows = 2 * orows

    def spot_of(step):
        b = lax.rem(me // 2 + steps // 2 + step, steps)
        return b, pl.multiple_of(b * srows, 8)

    def core_copy(d, step):
        layer = lax.rem(y + d, layers)
        _, at = spot_of(step)
        src = pl.multiple_of((layer * 2 + other) * grows + at, 8)
        return pltpu.make_async_remote_copy(
            src_ref=pv.at[pl.ds(src, srows), :],
            dst_ref=from_core.at[d, pl.ds(at, srows), :],
            send_sem=core_send.at[d, step],
            recv_sem=core_recv.at[d, step],
            device_id=(y * 2 + other, me),
            device_id_type=MESH,
        )

    def y_copy(d, step):
        layer = lax.rem(y + d, layers)
        _, at = spot_of(step)
        return pltpu.make_async_remote_copy(
            src_ref=kept.at[d, pl.ds(at, srows), :],
            dst_ref=from_y.at[d - 1, pl.ds(at, srows), :],
            send_sem=y_send.at[d - 1, step],
            recv_sem=y_recv.at[d - 1, step],
            device_id=(layer * 2 + core, me),
            device_id_type=MESH,
        )

    def pair_copy(d):
        to = lax.rem(me + d, owners)
        return pltpu.make_async_remote_copy(
            src_ref=summed.at[pl.ds(pl.multiple_of(to * orows, 8), orows), :],
            dst_ref=flat.at[pl.ds(pl.multiple_of(me * orows, 8), orows), :],
            send_sem=pair_send.at[d],
            recv_sem=pair_recv.at[d],
            device_id=(g, to),
            device_id_type=MESH,
        )

    order = list(range(1, layers)) + [0]
    for d in order:
        for step in range(steps):
            core_copy(d, step).start()
    for d in order:
        for step in range(steps):
            core_copy(d, step).wait_recv()
            _, at = spot_of(step)
            layer = lax.rem(y + d, layers)
            src = pl.multiple_of((layer * 2 + core) * grows + at, 8)
            here = pl.ds(at, srows)
            kept[d, here, :] = pv[pl.ds(src, srows), :] + from_core[d, here, :]
            if d:
                y_copy(d, step).start()

    for step in range(steps):
        b, at = spot_of(step)
        here = pl.ds(at, srows)
        total = kept[0, here, :]
        for d in range(1, layers):
            y_copy(d, step).wait_recv()
            total = total + from_y[d - 1, here, :]
        summed[here, :] = total
        for half in range(2):
            to = b * 2 + half

            @pl.when(to != me)
            def _():
                gap = lax.rem(to - me + owners, owners)
                pair_copy(gap).start()

    own = pl.ds(pl.multiple_of(me * orows, 8), orows)
    flat[own, :] = summed[own, :]
    for copy in small[1:]:
        copy.wait()
    cols = nsecond * nact
    c32[...] = cpad[...].astype(F32)

    def pick_row(i, carry):
        picked[pl.ds(i, 1), :] = c32[pl.ds(muv[i], 1), :]
        nu_col[pl.ds(i, 1), :] = jnp.broadcast_to(nuv[i], (1, LANES))
        return carry

    def act_row(i, carry):
        act_col[pl.ds(i, 1), :] = jnp.broadcast_to(actv[i], (1, LANES))
        return carry

    lax.fori_loop(0, all_rows, pick_row, 0)
    lax.fori_loop(0, nact, act_row, 0)
    section = section_of((1, cols), nact, nsecond)
    inside = lax.broadcasted_iota(jnp.int32, (1, cols), 1) - section * nact
    spread = inside == lax.broadcasted_iota(jnp.int32, (nact, cols), 0)
    wide = jnp.dot(
        picked[:, :nact].astype(BF16),
        jnp.where(spread, 1.0, 0.0).astype(BF16),
        preferred_element_type=F32,
    )
    amat_ref[...] = jnp.where(section == nu_col[:, :1], wide, 0.0).astype(BF16)
    act_wide = jnp.sum(
        jnp.where(spread, act_col[:, :1].astype(F32), 0.0), axis=0, keepdims=True
    ).astype(jnp.int32)
    ao_wide = jnp.zeros((1, cols), jnp.int32)
    for n in range(nsecond):
        ao_wide = jnp.where(section == n, aov[n], ao_wide)
    right_ref[...] = jnp.broadcast_to(jnp.bitwise_xor(act_wide, ao_wide), (8, cols))
    results = [
        pltpu.make_async_copy(src, dst, out_sem.at[k])
        for k, (src, dst) in enumerate(
            (
                (flat, flat_hbm),
                (amat_ref, amat_hbm),
                (right_ref, right_hbm),
                (act_col, act_out),
            )
        )
    ]
    for copy in results[1:]:
        copy.start()

    for d in range(1, owners):
        pair_copy(d).wait_recv()
    results[0].start()
    for d in order:
        for step in range(steps):
            core_copy(d, step).wait_send()
            if d:
                y_copy(d, step).wait_send()
    for d in range(1, owners):
        pair_copy(d).wait_send()
    for copy in results:
        copy.wait()


def finish_kernel(
    dims, flat_hbm, amat_hbm, right_hbm, act_in, out_hbm,
    flat, amat_ref, right_ref, act_col, out, in_sem, out_sem,
):
    owners, rows_dev, per_owner, nact = dims
    first = (lax.axis_index("grp") * owners + lax.axis_index("pair")) * per_owner
    arrived = [
        pltpu.make_async_copy(src, dst, in_sem.at[k])
        for k, (src, dst) in enumerate(
            (
                (flat_hbm, flat),
                (amat_hbm, amat_ref),
                (right_hbm, right_ref),
                (act_in, act_col),
            )
        )
    ]
    for copy in arrived:
        copy.start()
    for copy in arrived:
        copy.wait()
    weights = jnp.concatenate([amat_ref[...]] * 3, axis=0)
    right = right_ref[:1, :]
    copies = []
    for j in range(per_owner):
        f = jnp.concatenate(
            [
                flat[pl.ds((s * per_owner + j) * rows_dev, rows_dev), :]
                for s in range(owners)
            ],
            axis=0,
        )
        high = f.astype(BF16)
        rest = f - high.astype(F32)
        mid = rest.astype(BF16)
        low = (rest - mid.astype(F32)).astype(BF16)
        parts = jnp.concatenate([high, mid, low], axis=0).astype(F32).T[:nact].astype(BF16)
        full = jnp.dot(parts, weights, preferred_element_type=F32)
        p = first + j
        left = jnp.bitwise_xor(act_col[:, :1], act_col[pl.ds(p, 1), :1])
        here = pl.ds(j * nact, nact)
        out[here, :] = jnp.where(left == right, full, 0.0)
        copies.append(pltpu.make_async_copy(out.at[here, :], out_hbm.at[here, :], out_sem.at[j]))
        copies[-1].start()
    for copy in copies:
        copy.wait()


def fast(integrals, coeff, mu_index, nu_index, ao_irrep, act_irrep):
    rows_dev, slab, nbasis = integrals.shape
    nact = coeff.shape[1]
    groups, owners = lax.axis_size("grp"), lax.axis_size("pair")
    all_rows, nsecond = mu_index.shape[0], ao_irrep.shape[0]
    layers = groups // 2
    per_owner = nact // groups // owners
    grows = nact // groups * rows_dev
    cols = nsecond * nact
    rows = slab * rows_dev
    sizes = [rows // 5 // 16 * 16, rows * 8 // 25 // 16 * 16, rows * 8 // 25 // 16 * 16]
    sizes.append(rows - sum(sizes))
    chunks = tuple((sum(sizes[:k]), size) for k, size in enumerate(sizes))
    dims = (groups, owners, slab, rows_dev, nbasis, nact, nsecond, all_rows, chunks)
    span = -(-slab // 256) * 256
    x = integrals.transpose(1, 0, 2).reshape(rows, nbasis)
    steps = owners // 2
    hbm = pl.BlockSpec(memory_space=pltpu.HBM)
    tables = pl.pallas_call(
        functools.partial(transform_kernel, dims),
        out_shape=(
            jax.ShapeDtypeStruct((grows, LANES), F32),
            jax.ShapeDtypeStruct((all_rows, cols), BF16),
            jax.ShapeDtypeStruct((8, cols), jnp.int32),
            jax.ShapeDtypeStruct((nact, LANES), jnp.int32),
        ),
        in_specs=[hbm] * 6,
        out_specs=(hbm,) * 4,
        scratch_shapes=[
            pltpu.VMEM((rows, nbasis), BF16),
            pltpu.VMEM((LANES, nbasis), BF16),
            pltpu.VMEM((nact, span), BF16),
            pltpu.VMEM((nbasis, LANES), BF16),
            pltpu.VMEM((nbasis, LANES), F32),
            pltpu.VMEM((rows, LANES), F32),
            pltpu.VMEM((nact * rows_dev, LANES), F32),
            pltpu.SMEM((all_rows,), jnp.int32),
            pltpu.SMEM((all_rows,), jnp.int32),
            pltpu.SMEM((nsecond,), jnp.int32),
            pltpu.SMEM((nact,), jnp.int32),
            pltpu.VMEM((layers, grows, LANES), F32),
            pltpu.VMEM((layers, grows, LANES), F32),
            pltpu.VMEM((layers - 1, grows, LANES), F32),
            pltpu.VMEM((grows, LANES), F32),
            pltpu.VMEM((grows, LANES), F32),
            pltpu.VMEM((all_rows, LANES), F32),
            pltpu.VMEM((all_rows, LANES), jnp.int32),
            pltpu.VMEM((all_rows, cols), BF16),
            pltpu.VMEM((8, cols), jnp.int32),
            pltpu.VMEM((nact, LANES), jnp.int32),
            pltpu.SemaphoreType.DMA((4,)),
            pltpu.SemaphoreType.DMA((len(chunks),)),
            pltpu.SemaphoreType.DMA((5,)),
            pltpu.SemaphoreType.DMA((layers, steps)),
            pltpu.SemaphoreType.DMA((layers, steps)),
            pltpu.SemaphoreType.DMA((layers - 1, steps)),
            pltpu.SemaphoreType.DMA((layers - 1, steps)),
            pltpu.SemaphoreType.DMA((owners,)),
            pltpu.SemaphoreType.DMA((owners,)),
        ],
        compiler_params=pltpu.CompilerParams(
            collective_id=0, has_side_effects=True, vmem_limit_bytes=VMEM_LIMIT
        ),
        cost_estimate=pl.CostEstimate(
            flops=2 * rows * nbasis * nact, bytes_accessed=rows * nbasis * 2, transcendentals=0
        ),
    )(x, coeff.T, mu_index, nu_index, ao_irrep, act_irrep)
    return pl.pallas_call(
        functools.partial(finish_kernel, (owners, rows_dev, per_owner, nact)),
        out_shape=jax.ShapeDtypeStruct((per_owner * nact, cols), F32),
        in_specs=[hbm] * 4,
        out_specs=hbm,
        scratch_shapes=[
            pltpu.VMEM((grows, LANES), F32),
            pltpu.VMEM((all_rows, cols), BF16),
            pltpu.VMEM((8, cols), jnp.int32),
            pltpu.VMEM((nact, LANES), jnp.int32),
            pltpu.VMEM((per_owner * nact, cols), F32),
            pltpu.SemaphoreType.DMA((4,)),
            pltpu.SemaphoreType.DMA((per_owner,)),
        ],
        compiler_params=pltpu.CompilerParams(vmem_limit_bytes=VMEM_LIMIT),
    )(*tables)


def on_device(integrals, coeff, mu_index, nu_index, ao_irrep, act_irrep):
    rows_dev, slab, _ = integrals.shape
    nact = coeff.shape[1]
    groups, owners = lax.axis_size("grp"), lax.axis_size("pair")
    whole_rows = nact % (groups * owners) == 0
    fits = rows_dev == 8 and groups % 2 == 0 and groups > 2 and owners % 2 == 0
    if whole_rows and fits and slab * rows_dev % 16 == 0 and nact <= LANES:
        return fast(integrals, coeff, mu_index, nu_index, ao_irrep, act_irrep)
    return generic(integrals, coeff, mu_index, nu_index, ao_irrep, act_irrep)


def solution(mesh):
    in_specs = (P("pair", "grp", None), P(), P(), P(), P(), P())
    out_specs = P(("grp", "pair"), None)
    return jax.shard_map(
        on_device, mesh=mesh, in_specs=in_specs, out_specs=out_specs, check_vma=False
    )
```

```python
import functools

import jax
import jax.numpy as jnp
from jax import lax
from jax.experimental import pallas as pl
from jax.experimental.pallas import tpu as pltpu
from jax.sharding import PartitionSpec as P

MESH = pl.DeviceIdType.MESH
F32 = jnp.float32
BF16 = jnp.bfloat16
LANES = 128
VMEM_LIMIT = 64 * 1024 * 1024


def generic(integrals, coeff, mu_index, nu_index, ao_irrep, act_irrep):
    rows_dev, slab, nbasis = integrals.shape
    nactive = coeff.shape[1]
    groups = lax.axis_size("grp")
    owners = lax.axis_size("pair")
    total = nactive * nactive
    share = total // groups
    subset = share // owners
    all_rows = mu_index.shape[0]
    nsecond = ao_irrep.shape[0]
    slab_coeff = lax.dynamic_slice_in_dim(coeff, lax.axis_index("grp") * slab, slab, 0)
    rows_first = integrals.transpose(1, 0, 2).reshape(slab * rows_dev, nbasis)
    quarter = jnp.dot(rows_first, coeff, preferred_element_type=F32)
    quarter = quarter.astype(BF16).reshape(slab, rows_dev, nactive)
    partial_value = jnp.einsum("lp,lrq->rpq", slab_coeff, quarter, preferred_element_type=F32)
    partial_value = partial_value.reshape(rows_dev, total)
    mine = lax.psum_scatter(partial_value, "grp", scatter_dimension=1, tiled=True)
    picked = jnp.take(coeff, mu_index, axis=0).astype(F32)
    onehot = (nu_index[:, None] == jnp.arange(nsecond, dtype=jnp.int32)[None, :]).astype(F32)
    amat = (onehot[:, :, None] * picked[:, None, :]).reshape(all_rows, nsecond * nactive)
    sectioned = mine.reshape(rows_dev, owners, subset)
    arrived = lax.all_to_all(sectioned, "pair", split_axis=1, concat_axis=0, tiled=True)
    flat = arrived.reshape(all_rows, arrived.shape[2])
    full = lax.dot_general(flat, amat, (((0,), (0,)), ((), ())), precision=lax.Precision.HIGHEST)
    block_id = lax.axis_index("grp") * owners + lax.axis_index("pair")
    pair_ids = block_id * subset + jnp.arange(subset, dtype=jnp.int32)
    left_irrep = jnp.bitwise_xor(
        jnp.take(act_irrep, pair_ids // nactive), jnp.take(act_irrep, pair_ids % nactive)
    )
    col_ids = jnp.arange(nsecond * nactive, dtype=jnp.int32)
    right_irrep = jnp.bitwise_xor(
        jnp.take(ao_irrep, col_ids // nactive), jnp.take(act_irrep, col_ids % nactive)
    )
    allowed = left_irrep[:, None] == right_irrep[None, :]
    return jnp.where(allowed, full, jnp.zeros_like(full))


def section_of(shape, nactive, nsecond):
    col = lax.broadcasted_iota(jnp.int32, shape, 1)
    section = jnp.zeros(shape, jnp.int32)
    for n in range(1, nsecond):
        section = section + jnp.where(col >= n * nactive, 1, 0)
    return section


def transform_kernel(
    dims, x_hbm, c_hbm, mu_hbm, nu_hbm, ao_hbm, act_hbm, flat_hbm, amat_hbm, right_hbm, act_out,
    xv, cv, st, cpad, c32, qv, pv, muv, nuv, aov, actv, from_core, kept, from_y, summed, flat,
    picked, nu_col, amat_ref, right_ref, act_col, out_sem, x_sem, in_sem, core_send, core_recv, y_send, y_recv, pair_send, pair_recv,
):
    groups, owners, slab, rows_dev, nbasis, nact, nsecond, all_rows, chunk, early = dims
    layers = groups // 2
    per_group = nact // groups
    per_owner = per_group // owners
    grows = per_group * rows_dev
    orows = per_owner * rows_dev
    g = lax.axis_index("grp")
    me = lax.axis_index("pair")
    y, core = g // 2, g % 2
    other = 1 - core
    nchunks = slab * rows_dev // chunk

    small = [
        pltpu.make_async_copy(src, dst, in_sem.at[k])
        for k, (src, dst) in enumerate(
            ((c_hbm, cv.at[pl.ds(0, nact), :]), (mu_hbm, muv), (nu_hbm, nuv), (ao_hbm, aov), (act_hbm, actv))
        )
    ]
    small[0].start()

    def x_copy(k):
        where = pl.ds(pl.multiple_of(k * chunk, 16), chunk)
        return pltpu.make_async_copy(x_hbm.at[where, :], xv.at[where, :], x_sem.at[k])

    for k in range(nchunks):
        x_copy(k).start()
    for copy in small[1:]:
        copy.start()

    barrier = pltpu.get_barrier_semaphore()
    pl.semaphore_signal(barrier, inc=1, device_id=(y * 2 + other, me), device_id_type=MESH)
    for d in range(1, layers):
        yy = lax.rem(y + d, layers)
        pl.semaphore_signal(barrier, inc=1, device_id=(yy * 2 + core, me), device_id_type=MESH)
    for d in range(1, owners):
        pl.semaphore_signal(
            barrier, inc=1, device_id=(g, lax.rem(me + d, owners)), device_id_type=MESH
        )

    cv[nact:, :] = jnp.zeros((LANES - nact, nbasis), BF16)
    small[0].wait()
    cpad[...] = cv[...].T


    def quarter_step(k, carry):
        x_copy(k).wait()
        where = pl.ds(pl.multiple_of(k * chunk, 16), chunk)
        qv[where, :] = jnp.dot(xv[where, :], cpad[...], preferred_element_type=F32)
        return carry

    def half_part(first, count, fresh):
        for i in range(0, rows_dev, 2):
            q = jnp.concatenate(
                [
                    qv[pl.ds(first * rows_dev + i + k, count, stride=rows_dev), :].astype(BF16)
                    for k in range(2)
                ],
                axis=1,
            )
            part = jnp.dot(st[:, first : first + count], q, preferred_element_type=F32)
            for k in range(2):
                spot = pl.ds(i + k, nact, stride=rows_dev)
                mine = part[:, k * LANES : (k + 1) * LANES]
                pv[spot, :] = mine if fresh else pv[spot, :] + mine

    lax.fori_loop(0, early, quarter_step, 0)
    for part in range(groups):

        @pl.when(g == part)
        def _():
            st[:, :slab] = cv[:nact, part * slab : (part + 1) * slab]

    cut = early * chunk // rows_dev // 256 * 256
    if cut:
        half_part(0, cut, True)
    lax.fori_loop(early, nchunks, quarter_step, 0)
    half_part(cut, slab - cut, not cut)

    pl.semaphore_wait(barrier, layers + owners - 1)

    steps = owners // 2
    srows = 2 * orows

    def spot_of(step):
        b = lax.rem(me // 2 + steps // 2 + step, steps)
        return b, pl.multiple_of(b * srows, 8)

    def core_copy(d, step):
        layer = lax.rem(y + d, layers)
        _, at = spot_of(step)
        src = pl.multiple_of((layer * 2 + other) * grows + at, 8)
        return pltpu.make_async_remote_copy(
            src_ref=pv.at[pl.ds(src, srows), :],
            dst_ref=from_core.at[d, pl.ds(at, srows), :],
            send_sem=core_send.at[d, step],
            recv_sem=core_recv.at[d, step],
            device_id=(y * 2 + other, me),
            device_id_type=MESH,
        )

    def y_copy(d, step):
        layer = lax.rem(y + d, layers)
        _, at = spot_of(step)
        return pltpu.make_async_remote_copy(
            src_ref=kept.at[d, pl.ds(at, srows), :],
            dst_ref=from_y.at[d - 1, pl.ds(at, srows), :],
            send_sem=y_send.at[d - 1, step],
            recv_sem=y_recv.at[d - 1, step],
            device_id=(layer * 2 + core, me),
            device_id_type=MESH,
        )

    def pair_copy(d):
        to = lax.rem(me + d, owners)
        return pltpu.make_async_remote_copy(
            src_ref=summed.at[pl.ds(pl.multiple_of(to * orows, 8), orows), :],
            dst_ref=flat.at[pl.ds(pl.multiple_of(me * orows, 8), orows), :],
            send_sem=pair_send.at[d],
            recv_sem=pair_recv.at[d],
            device_id=(g, to),
            device_id_type=MESH,
        )

    order = list(range(1, layers)) + [0]
    for d in order:
        for step in range(steps):
            core_copy(d, step).start()
    for d in order:
        for step in range(steps):
            core_copy(d, step).wait_recv()
            _, at = spot_of(step)
            layer = lax.rem(y + d, layers)
            src = pl.multiple_of((layer * 2 + core) * grows + at, 8)
            here = pl.ds(at, srows)
            kept[d, here, :] = pv[pl.ds(src, srows), :] + from_core[d, here, :]
            if d:
                y_copy(d, step).start()

    for step in range(steps):
        b, at = spot_of(step)
        here = pl.ds(at, srows)
        total = kept[0, here, :]
        for d in range(1, layers):
            y_copy(d, step).wait_recv()
            total = total + from_y[d - 1, here, :]
        summed[here, :] = total
        for half in range(2):
            to = b * 2 + half

            @pl.when(to != me)
            def _():
                gap = lax.rem(to - me + owners, owners)
                pair_copy(gap).start()

    own = pl.ds(pl.multiple_of(me * orows, 8), orows)
    flat[own, :] = summed[own, :]
    for copy in small[1:]:
        copy.wait()
    cols = nsecond * nact
    c32[...] = cpad[...].astype(F32)

    def pick_row(i, carry):
        picked[pl.ds(i, 1), :] = c32[pl.ds(muv[i], 1), :]
        nu_col[pl.ds(i, 1), :] = jnp.broadcast_to(nuv[i], (1, LANES))
        return carry

    def act_row(i, carry):
        act_col[pl.ds(i, 1), :] = jnp.broadcast_to(actv[i], (1, LANES))
        return carry

    lax.fori_loop(0, all_rows, pick_row, 0)
    lax.fori_loop(0, nact, act_row, 0)
    section = section_of((1, cols), nact, nsecond)
    inside = lax.broadcasted_iota(jnp.int32, (1, cols), 1) - section * nact
    spread = inside == lax.broadcasted_iota(jnp.int32, (nact, cols), 0)
    wide = jnp.dot(
        picked[:, :nact].astype(BF16),
        jnp.where(spread, 1.0, 0.0).astype(BF16),
        preferred_element_type=F32,
    )
    amat_ref[...] = jnp.where(section == nu_col[:, :1], wide, 0.0).astype(BF16)
    act_wide = jnp.sum(
        jnp.where(spread, act_col[:, :1].astype(F32), 0.0), axis=0, keepdims=True
    ).astype(jnp.int32)
    ao_wide = jnp.zeros((1, cols), jnp.int32)
    for n in range(nsecond):
        ao_wide = jnp.where(section == n, aov[n], ao_wide)
    right_ref[...] = jnp.broadcast_to(jnp.bitwise_xor(act_wide, ao_wide), (8, cols))
    results = [
        pltpu.make_async_copy(src, dst, out_sem.at[k])
        for k, (src, dst) in enumerate(
            (
                (flat, flat_hbm),
                (amat_ref, amat_hbm),
                (right_ref, right_hbm),
                (act_col, act_out),
            )
        )
    ]
    for copy in results[1:]:
        copy.start()

    for d in range(1, owners):
        pair_copy(d).wait_recv()
    results[0].start()
    for d in order:
        for step in range(steps):
            core_copy(d, step).wait_send()
            if d:
                y_copy(d, step).wait_send()
    for d in range(1, owners):
        pair_copy(d).wait_send()
    for copy in results:
        copy.wait()


def finish_kernel(
    dims, flat_hbm, amat_hbm, right_hbm, act_in, out_hbm,
    flat, amat_ref, right_ref, act_col, out, in_sem, out_sem,
):
    owners, rows_dev, per_owner, nact = dims
    first = (lax.axis_index("grp") * owners + lax.axis_index("pair")) * per_owner
    arrived = [
        pltpu.make_async_copy(src, dst, in_sem.at[k])
        for k, (src, dst) in enumerate(
            (
                (flat_hbm, flat),
                (amat_hbm, amat_ref),
                (right_hbm, right_ref),
                (act_in, act_col),
            )
        )
    ]
    for copy in arrived:
        copy.start()
    for copy in arrived:
        copy.wait()
    weights = jnp.concatenate([amat_ref[...]] * 3, axis=0)
    right = right_ref[:1, :]
    copies = []
    for j in range(per_owner):
        f = jnp.concatenate(
            [
                flat[pl.ds((s * per_owner + j) * rows_dev, rows_dev), :]
                for s in range(owners)
            ],
            axis=0,
        )
        high = f.astype(BF16)
        rest = f - high.astype(F32)
        mid = rest.astype(BF16)
        low = (rest - mid.astype(F32)).astype(BF16)
        parts = jnp.concatenate([high, mid, low], axis=0).astype(F32).T[:nact].astype(BF16)
        full = jnp.dot(parts, weights, preferred_element_type=F32)
        p = first + j
        left = jnp.bitwise_xor(act_col[:, :1], act_col[pl.ds(p, 1), :1])
        here = pl.ds(j * nact, nact)
        out[here, :] = jnp.where(left == right, full, 0.0)
        copies.append(pltpu.make_async_copy(out.at[here, :], out_hbm.at[here, :], out_sem.at[j]))
        copies[-1].start()
    for copy in copies:
        copy.wait()


def fast(integrals, coeff, mu_index, nu_index, ao_irrep, act_irrep):
    rows_dev, slab, nbasis = integrals.shape
    nact = coeff.shape[1]
    groups, owners = lax.axis_size("grp"), lax.axis_size("pair")
    all_rows, nsecond = mu_index.shape[0], ao_irrep.shape[0]
    layers = groups // 2
    per_owner = nact // groups // owners
    grows = nact // groups * rows_dev
    cols = nsecond * nact
    rows = slab * rows_dev
    chunk = max(c for c in range(16, 401, 16) if rows % c == 0)
    nchunks = rows // chunk
    early = min(nchunks, -(-256 * rows_dev // chunk))
    dims = (groups, owners, slab, rows_dev, nbasis, nact, nsecond, all_rows, chunk, early)
    span = -(-slab // 256) * 256
    x = integrals.transpose(1, 0, 2).reshape(rows, nbasis)
    steps = owners // 2
    hbm = pl.BlockSpec(memory_space=pltpu.HBM)
    tables = pl.pallas_call(
        functools.partial(transform_kernel, dims),
        out_shape=(
            jax.ShapeDtypeStruct((grows, LANES), F32),
            jax.ShapeDtypeStruct((all_rows, cols), BF16),
            jax.ShapeDtypeStruct((8, cols), jnp.int32),
            jax.ShapeDtypeStruct((nact, LANES), jnp.int32),
        ),
        in_specs=[hbm] * 6,
        out_specs=(hbm,) * 4,
        scratch_shapes=[
            pltpu.VMEM((rows, nbasis), BF16),
            pltpu.VMEM((LANES, nbasis), BF16),
            pltpu.VMEM((nact, span), BF16),
            pltpu.VMEM((nbasis, LANES), BF16),
            pltpu.VMEM((nbasis, LANES), F32),
            pltpu.VMEM((rows, LANES), F32),
            pltpu.VMEM((nact * rows_dev, LANES), F32),
            pltpu.SMEM((all_rows,), jnp.int32),
            pltpu.SMEM((all_rows,), jnp.int32),
            pltpu.SMEM((nsecond,), jnp.int32),
            pltpu.SMEM((nact,), jnp.int32),
            pltpu.VMEM((layers, grows, LANES), F32),
            pltpu.VMEM((layers, grows, LANES), F32),
            pltpu.VMEM((layers - 1, grows, LANES), F32),
            pltpu.VMEM((grows, LANES), F32),
            pltpu.VMEM((grows, LANES), F32),
            pltpu.VMEM((all_rows, LANES), F32),
            pltpu.VMEM((all_rows, LANES), jnp.int32),
            pltpu.VMEM((all_rows, cols), BF16),
            pltpu.VMEM((8, cols), jnp.int32),
            pltpu.VMEM((nact, LANES), jnp.int32),
            pltpu.SemaphoreType.DMA((4,)),
            pltpu.SemaphoreType.DMA((nchunks,)),
            pltpu.SemaphoreType.DMA((5,)),
            pltpu.SemaphoreType.DMA((layers, steps)),
            pltpu.SemaphoreType.DMA((layers, steps)),
            pltpu.SemaphoreType.DMA((layers - 1, steps)),
            pltpu.SemaphoreType.DMA((layers - 1, steps)),
            pltpu.SemaphoreType.DMA((owners,)),
            pltpu.SemaphoreType.DMA((owners,)),
        ],
        compiler_params=pltpu.CompilerParams(
            collective_id=0, has_side_effects=True, vmem_limit_bytes=VMEM_LIMIT
        ),
        cost_estimate=pl.CostEstimate(
            flops=2 * rows * nbasis * nact, bytes_accessed=rows * nbasis * 2, transcendentals=0
        ),
    )(x, coeff.T, mu_index, nu_index, ao_irrep, act_irrep)
    return pl.pallas_call(
        functools.partial(finish_kernel, (owners, rows_dev, per_owner, nact)),
        out_shape=jax.ShapeDtypeStruct((per_owner * nact, cols), F32),
        in_specs=[hbm] * 4,
        out_specs=hbm,
        scratch_shapes=[
            pltpu.VMEM((grows, LANES), F32),
            pltpu.VMEM((all_rows, cols), BF16),
            pltpu.VMEM((8, cols), jnp.int32),
            pltpu.VMEM((nact, LANES), jnp.int32),
            pltpu.VMEM((per_owner * nact, cols), F32),
            pltpu.SemaphoreType.DMA((4,)),
            pltpu.SemaphoreType.DMA((per_owner,)),
        ],
        compiler_params=pltpu.CompilerParams(vmem_limit_bytes=VMEM_LIMIT),
    )(*tables)


def on_device(integrals, coeff, mu_index, nu_index, ao_irrep, act_irrep):
    rows_dev, slab, _ = integrals.shape
    nact = coeff.shape[1]
    groups, owners = lax.axis_size("grp"), lax.axis_size("pair")
    whole_rows = nact % (groups * owners) == 0
    fits = rows_dev == 8 and groups % 2 == 0 and groups > 2 and owners % 2 == 0
    if whole_rows and fits and slab * rows_dev % 16 == 0 and nact <= LANES:
        return fast(integrals, coeff, mu_index, nu_index, ao_irrep, act_irrep)
    return generic(integrals, coeff, mu_index, nu_index, ao_irrep, act_irrep)


def solution(mesh):
    in_specs = (P("pair", "grp", None), P(), P(), P(), P(), P())
    out_specs = P(("grp", "pair"), None)
    return jax.shard_map(
        on_device, mesh=mesh, in_specs=in_specs, out_specs=out_specs, check_vma=False
    )
```

```python
import functools

import jax
import jax.numpy as jnp
from jax import lax
from jax.experimental import pallas as pl
from jax.experimental.pallas import tpu as pltpu
from jax.sharding import PartitionSpec as P

MESH = pl.DeviceIdType.MESH
F32 = jnp.float32
BF16 = jnp.bfloat16
LANES = 128
AHEAD = 3
VMEM_LIMIT = 64 * 1024 * 1024


def generic(integrals, coeff, mu_index, nu_index, ao_irrep, act_irrep):
    rows_dev, slab, nbasis = integrals.shape
    nactive = coeff.shape[1]
    groups = lax.axis_size("grp")
    owners = lax.axis_size("pair")
    total = nactive * nactive
    share = total // groups
    subset = share // owners
    all_rows = mu_index.shape[0]
    nsecond = ao_irrep.shape[0]
    slab_coeff = lax.dynamic_slice_in_dim(coeff, lax.axis_index("grp") * slab, slab, 0)
    rows_first = integrals.transpose(1, 0, 2).reshape(slab * rows_dev, nbasis)
    quarter = jnp.dot(rows_first, coeff, preferred_element_type=F32)
    quarter = quarter.astype(BF16).reshape(slab, rows_dev, nactive)
    partial_value = jnp.einsum("lp,lrq->rpq", slab_coeff, quarter, preferred_element_type=F32)
    partial_value = partial_value.reshape(rows_dev, total)
    mine = lax.psum_scatter(partial_value, "grp", scatter_dimension=1, tiled=True)
    picked = jnp.take(coeff, mu_index, axis=0).astype(F32)
    onehot = (nu_index[:, None] == jnp.arange(nsecond, dtype=jnp.int32)[None, :]).astype(F32)
    amat = (onehot[:, :, None] * picked[:, None, :]).reshape(all_rows, nsecond * nactive)
    sectioned = mine.reshape(rows_dev, owners, subset)
    arrived = lax.all_to_all(sectioned, "pair", split_axis=1, concat_axis=0, tiled=True)
    flat = arrived.reshape(all_rows, arrived.shape[2])
    full = lax.dot_general(flat, amat, (((0,), (0,)), ((), ())), precision=lax.Precision.HIGHEST)
    block_id = lax.axis_index("grp") * owners + lax.axis_index("pair")
    pair_ids = block_id * subset + jnp.arange(subset, dtype=jnp.int32)
    left_irrep = jnp.bitwise_xor(
        jnp.take(act_irrep, pair_ids // nactive), jnp.take(act_irrep, pair_ids % nactive)
    )
    col_ids = jnp.arange(nsecond * nactive, dtype=jnp.int32)
    right_irrep = jnp.bitwise_xor(
        jnp.take(ao_irrep, col_ids // nactive), jnp.take(act_irrep, col_ids % nactive)
    )
    allowed = left_irrep[:, None] == right_irrep[None, :]
    return jnp.where(allowed, full, jnp.zeros_like(full))


def section_of(shape, nactive, nsecond):
    col = lax.broadcasted_iota(jnp.int32, shape, 1)
    section = jnp.zeros(shape, jnp.int32)
    for n in range(1, nsecond):
        section = section + jnp.where(col >= n * nactive, 1, 0)
    return section


def transform_kernel(
    dims, x_hbm, c_hbm, mu_hbm, nu_hbm, ao_hbm, act_hbm, flat_hbm, amat_hbm, right_hbm, act_out,
    xv, cv, st, cpad, c32, qv, pv, muv, nuv, aov, actv, from_core, kept, from_y, summed, flat,
    picked, nu_col, amat_ref, right_ref, act_col, out_sem, x_sem, in_sem, core_send, core_recv, y_send, y_recv, pair_send, pair_recv,
):
    groups, owners, slab, rows_dev, nbasis, nact, nsecond, all_rows, chunk, early = dims
    layers = groups // 2
    per_group = nact // groups
    per_owner = per_group // owners
    grows = per_group * rows_dev
    orows = per_owner * rows_dev
    g = lax.axis_index("grp")
    me = lax.axis_index("pair")
    y, core = g // 2, g % 2
    other = 1 - core
    nchunks = slab * rows_dev // chunk

    small = [
        pltpu.make_async_copy(src, dst, in_sem.at[k])
        for k, (src, dst) in enumerate(
            ((c_hbm, cv.at[pl.ds(0, nact), :]), (mu_hbm, muv), (nu_hbm, nuv), (ao_hbm, aov), (act_hbm, actv))
        )
    ]
    small[0].start()

    def x_copy(k):
        where = pl.ds(pl.multiple_of(k * chunk, 16), chunk)
        return pltpu.make_async_copy(x_hbm.at[where, :], xv.at[where, :], x_sem.at[k])

    for k in range(min(AHEAD, nchunks)):
        x_copy(k).start()
    for copy in small[1:]:
        copy.start()

    barrier = pltpu.get_barrier_semaphore()
    pl.semaphore_signal(barrier, inc=1, device_id=(y * 2 + other, me), device_id_type=MESH)
    for d in range(1, layers):
        yy = lax.rem(y + d, layers)
        pl.semaphore_signal(barrier, inc=1, device_id=(yy * 2 + core, me), device_id_type=MESH)
    for d in range(1, owners):
        pl.semaphore_signal(
            barrier, inc=1, device_id=(g, lax.rem(me + d, owners)), device_id_type=MESH
        )

    cv[nact:, :] = jnp.zeros((LANES - nact, nbasis), BF16)
    small[0].wait()
    cpad[...] = cv[...].T


    def quarter_step(k, carry):
        x_copy(k).wait()

        @pl.when(k + AHEAD < nchunks)
        def _():
            x_copy(k + AHEAD).start()

        where = pl.ds(pl.multiple_of(k * chunk, 16), chunk)
        qv[where, :] = jnp.dot(xv[where, :], cpad[...], preferred_element_type=F32)
        return carry

    def half_part(first, count, fresh):
        for i in range(0, rows_dev, 2):
            q = jnp.concatenate(
                [
                    qv[pl.ds(first * rows_dev + i + k, count, stride=rows_dev), :].astype(BF16)
                    for k in range(2)
                ],
                axis=1,
            )
            part = jnp.dot(st[:, first : first + count], q, preferred_element_type=F32)
            for k in range(2):
                spot = pl.ds(i + k, nact, stride=rows_dev)
                mine = part[:, k * LANES : (k + 1) * LANES]
                pv[spot, :] = mine if fresh else pv[spot, :] + mine

    lax.fori_loop(0, early, quarter_step, 0)
    for part in range(groups):

        @pl.when(g == part)
        def _():
            st[:, :slab] = cv[:nact, part * slab : (part + 1) * slab]

    cut = early * chunk // rows_dev // 256 * 256
    if cut:
        half_part(0, cut, True)
    lax.fori_loop(early, nchunks, quarter_step, 0)
    half_part(cut, slab - cut, not cut)

    pl.semaphore_wait(barrier, layers + owners - 1)

    steps = owners // 2
    srows = 2 * orows

    def spot_of(step):
        b = lax.rem(me // 2 + steps // 2 + step, steps)
        return b, pl.multiple_of(b * srows, 8)

    def core_copy(d, step):
        layer = lax.rem(y + d, layers)
        _, at = spot_of(step)
        src = pl.multiple_of((layer * 2 + other) * grows + at, 8)
        return pltpu.make_async_remote_copy(
            src_ref=pv.at[pl.ds(src, srows), :],
            dst_ref=from_core.at[d, pl.ds(at, srows), :],
            send_sem=core_send.at[d, step],
            recv_sem=core_recv.at[d, step],
            device_id=(y * 2 + other, me),
            device_id_type=MESH,
        )

    def y_copy(d, step):
        layer = lax.rem(y + d, layers)
        _, at = spot_of(step)
        return pltpu.make_async_remote_copy(
            src_ref=kept.at[d, pl.ds(at, srows), :],
            dst_ref=from_y.at[d - 1, pl.ds(at, srows), :],
            send_sem=y_send.at[d - 1, step],
            recv_sem=y_recv.at[d - 1, step],
            device_id=(layer * 2 + core, me),
            device_id_type=MESH,
        )

    def pair_copy(d):
        to = lax.rem(me + d, owners)
        return pltpu.make_async_remote_copy(
            src_ref=summed.at[pl.ds(pl.multiple_of(to * orows, 8), orows), :],
            dst_ref=flat.at[pl.ds(pl.multiple_of(me * orows, 8), orows), :],
            send_sem=pair_send.at[d],
            recv_sem=pair_recv.at[d],
            device_id=(g, to),
            device_id_type=MESH,
        )

    order = list(range(1, layers)) + [0]
    for d in order:
        for step in range(steps):
            core_copy(d, step).start()
    for d in order:
        for step in range(steps):
            core_copy(d, step).wait_recv()
            _, at = spot_of(step)
            layer = lax.rem(y + d, layers)
            src = pl.multiple_of((layer * 2 + core) * grows + at, 8)
            here = pl.ds(at, srows)
            kept[d, here, :] = pv[pl.ds(src, srows), :] + from_core[d, here, :]
            if d:
                y_copy(d, step).start()

    for step in range(steps):
        b, at = spot_of(step)
        here = pl.ds(at, srows)
        total = kept[0, here, :]
        for d in range(1, layers):
            y_copy(d, step).wait_recv()
            total = total + from_y[d - 1, here, :]
        summed[here, :] = total
        for half in range(2):
            to = b * 2 + half

            @pl.when(to != me)
            def _():
                gap = lax.rem(to - me + owners, owners)
                pair_copy(gap).start()

    own = pl.ds(pl.multiple_of(me * orows, 8), orows)
    flat[own, :] = summed[own, :]
    for copy in small[1:]:
        copy.wait()
    cols = nsecond * nact
    c32[...] = cpad[...].astype(F32)

    def pick_row(i, carry):
        picked[pl.ds(i, 1), :] = c32[pl.ds(muv[i], 1), :]
        nu_col[pl.ds(i, 1), :] = jnp.broadcast_to(nuv[i], (1, LANES))
        return carry

    def act_row(i, carry):
        act_col[pl.ds(i, 1), :] = jnp.broadcast_to(actv[i], (1, LANES))
        return carry

    lax.fori_loop(0, all_rows, pick_row, 0)
    lax.fori_loop(0, nact, act_row, 0)
    section = section_of((1, cols), nact, nsecond)
    inside = lax.broadcasted_iota(jnp.int32, (1, cols), 1) - section * nact
    spread = inside == lax.broadcasted_iota(jnp.int32, (nact, cols), 0)
    wide = jnp.dot(
        picked[:, :nact].astype(BF16),
        jnp.where(spread, 1.0, 0.0).astype(BF16),
        preferred_element_type=F32,
    )
    amat_ref[...] = jnp.where(section == nu_col[:, :1], wide, 0.0).astype(BF16)
    act_wide = jnp.sum(
        jnp.where(spread, act_col[:, :1].astype(F32), 0.0), axis=0, keepdims=True
    ).astype(jnp.int32)
    ao_wide = jnp.zeros((1, cols), jnp.int32)
    for n in range(nsecond):
        ao_wide = jnp.where(section == n, aov[n], ao_wide)
    right_ref[...] = jnp.broadcast_to(jnp.bitwise_xor(act_wide, ao_wide), (8, cols))
    results = [
        pltpu.make_async_copy(src, dst, out_sem.at[k])
        for k, (src, dst) in enumerate(
            (
                (flat, flat_hbm),
                (amat_ref, amat_hbm),
                (right_ref, right_hbm),
                (act_col, act_out),
            )
        )
    ]
    for copy in results[1:]:
        copy.start()

    for d in range(1, owners):
        pair_copy(d).wait_recv()
    results[0].start()
    for d in order:
        for step in range(steps):
            core_copy(d, step).wait_send()
            if d:
                y_copy(d, step).wait_send()
    for d in range(1, owners):
        pair_copy(d).wait_send()
    for copy in results:
        copy.wait()


def finish_kernel(
    dims, flat_hbm, amat_hbm, right_hbm, act_in, out_hbm,
    flat, amat_ref, right_ref, act_col, out, in_sem, out_sem,
):
    owners, rows_dev, per_owner, nact = dims
    first = (lax.axis_index("grp") * owners + lax.axis_index("pair")) * per_owner
    arrived = [
        pltpu.make_async_copy(src, dst, in_sem.at[k])
        for k, (src, dst) in enumerate(
            (
                (flat_hbm, flat),
                (amat_hbm, amat_ref),
                (right_hbm, right_ref),
                (act_in, act_col),
            )
        )
    ]
    for copy in arrived:
        copy.start()
    for copy in arrived:
        copy.wait()
    weights = jnp.concatenate([amat_ref[...]] * 3, axis=0)
    right = right_ref[:1, :]
    copies = []
    for j in range(per_owner):
        f = jnp.concatenate(
            [
                flat[pl.ds((s * per_owner + j) * rows_dev, rows_dev), :]
                for s in range(owners)
            ],
            axis=0,
        )
        high = f.astype(BF16)
        rest = f - high.astype(F32)
        mid = rest.astype(BF16)
        low = (rest - mid.astype(F32)).astype(BF16)
        parts = jnp.concatenate([high, mid, low], axis=0).astype(F32).T[:nact].astype(BF16)
        full = jnp.dot(parts, weights, preferred_element_type=F32)
        p = first + j
        left = jnp.bitwise_xor(act_col[:, :1], act_col[pl.ds(p, 1), :1])
        here = pl.ds(j * nact, nact)
        out[here, :] = jnp.where(left == right, full, 0.0)
        copies.append(pltpu.make_async_copy(out.at[here, :], out_hbm.at[here, :], out_sem.at[j]))
        copies[-1].start()
    for copy in copies:
        copy.wait()


def fast(integrals, coeff, mu_index, nu_index, ao_irrep, act_irrep):
    rows_dev, slab, nbasis = integrals.shape
    nact = coeff.shape[1]
    groups, owners = lax.axis_size("grp"), lax.axis_size("pair")
    all_rows, nsecond = mu_index.shape[0], ao_irrep.shape[0]
    layers = groups // 2
    per_owner = nact // groups // owners
    grows = nact // groups * rows_dev
    cols = nsecond * nact
    rows = slab * rows_dev
    chunk = max(c for c in range(16, 401, 16) if rows % c == 0)
    nchunks = rows // chunk
    early = min(nchunks, -(-256 * rows_dev // chunk))
    dims = (groups, owners, slab, rows_dev, nbasis, nact, nsecond, all_rows, chunk, early)
    span = -(-slab // 256) * 256
    x = integrals.transpose(1, 0, 2).reshape(rows, nbasis)
    steps = owners // 2
    hbm = pl.BlockSpec(memory_space=pltpu.HBM)
    tables = pl.pallas_call(
        functools.partial(transform_kernel, dims),
        out_shape=(
            jax.ShapeDtypeStruct((grows, LANES), F32),
            jax.ShapeDtypeStruct((all_rows, cols), BF16),
            jax.ShapeDtypeStruct((8, cols), jnp.int32),
            jax.ShapeDtypeStruct((nact, LANES), jnp.int32),
        ),
        in_specs=[hbm] * 6,
        out_specs=(hbm,) * 4,
        scratch_shapes=[
            pltpu.VMEM((rows, nbasis), BF16),
            pltpu.VMEM((LANES, nbasis), BF16),
            pltpu.VMEM((nact, span), BF16),
            pltpu.VMEM((nbasis, LANES), BF16),
            pltpu.VMEM((nbasis, LANES), F32),
            pltpu.VMEM((rows, LANES), F32),
            pltpu.VMEM((nact * rows_dev, LANES), F32),
            pltpu.SMEM((all_rows,), jnp.int32),
            pltpu.SMEM((all_rows,), jnp.int32),
            pltpu.SMEM((nsecond,), jnp.int32),
            pltpu.SMEM((nact,), jnp.int32),
            pltpu.VMEM((layers, grows, LANES), F32),
            pltpu.VMEM((layers, grows, LANES), F32),
            pltpu.VMEM((layers - 1, grows, LANES), F32),
            pltpu.VMEM((grows, LANES), F32),
            pltpu.VMEM((grows, LANES), F32),
            pltpu.VMEM((all_rows, LANES), F32),
            pltpu.VMEM((all_rows, LANES), jnp.int32),
            pltpu.VMEM((all_rows, cols), BF16),
            pltpu.VMEM((8, cols), jnp.int32),
            pltpu.VMEM((nact, LANES), jnp.int32),
            pltpu.SemaphoreType.DMA((4,)),
            pltpu.SemaphoreType.DMA((nchunks,)),
            pltpu.SemaphoreType.DMA((5,)),
            pltpu.SemaphoreType.DMA((layers, steps)),
            pltpu.SemaphoreType.DMA((layers, steps)),
            pltpu.SemaphoreType.DMA((layers - 1, steps)),
            pltpu.SemaphoreType.DMA((layers - 1, steps)),
            pltpu.SemaphoreType.DMA((owners,)),
            pltpu.SemaphoreType.DMA((owners,)),
        ],
        compiler_params=pltpu.CompilerParams(
            collective_id=0, has_side_effects=True, vmem_limit_bytes=VMEM_LIMIT
        ),
        cost_estimate=pl.CostEstimate(
            flops=2 * rows * nbasis * nact, bytes_accessed=rows * nbasis * 2, transcendentals=0
        ),
    )(x, coeff.T, mu_index, nu_index, ao_irrep, act_irrep)
    return pl.pallas_call(
        functools.partial(finish_kernel, (owners, rows_dev, per_owner, nact)),
        out_shape=jax.ShapeDtypeStruct((per_owner * nact, cols), F32),
        in_specs=[hbm] * 4,
        out_specs=hbm,
        scratch_shapes=[
            pltpu.VMEM((grows, LANES), F32),
            pltpu.VMEM((all_rows, cols), BF16),
            pltpu.VMEM((8, cols), jnp.int32),
            pltpu.VMEM((nact, LANES), jnp.int32),
            pltpu.VMEM((per_owner * nact, cols), F32),
            pltpu.SemaphoreType.DMA((4,)),
            pltpu.SemaphoreType.DMA((per_owner,)),
        ],
        compiler_params=pltpu.CompilerParams(vmem_limit_bytes=VMEM_LIMIT),
    )(*tables)


def on_device(integrals, coeff, mu_index, nu_index, ao_irrep, act_irrep):
    rows_dev, slab, _ = integrals.shape
    nact = coeff.shape[1]
    groups, owners = lax.axis_size("grp"), lax.axis_size("pair")
    whole_rows = nact % (groups * owners) == 0
    fits = rows_dev == 8 and groups % 2 == 0 and groups > 2 and owners % 2 == 0
    if whole_rows and fits and slab * rows_dev % 16 == 0 and nact <= LANES:
        return fast(integrals, coeff, mu_index, nu_index, ao_irrep, act_irrep)
    return generic(integrals, coeff, mu_index, nu_index, ao_irrep, act_irrep)


def solution(mesh):
    in_specs = (P("pair", "grp", None), P(), P(), P(), P(), P())
    out_specs = P(("grp", "pair"), None)
    return jax.shard_map(
        on_device, mesh=mesh, in_specs=in_specs, out_specs=out_specs, check_vma=False
    )
```

```python
import functools

import jax
import jax.numpy as jnp
from jax import lax
from jax.experimental import pallas as pl
from jax.experimental.pallas import tpu as pltpu
from jax.sharding import PartitionSpec as P

MESH = pl.DeviceIdType.MESH
F32 = jnp.float32
BF16 = jnp.bfloat16
LANES = 128
AHEAD = 2
VMEM_LIMIT = 64 * 1024 * 1024


def generic(integrals, coeff, mu_index, nu_index, ao_irrep, act_irrep):
    rows_dev, slab, nbasis = integrals.shape
    nactive = coeff.shape[1]
    groups = lax.axis_size("grp")
    owners = lax.axis_size("pair")
    total = nactive * nactive
    share = total // groups
    subset = share // owners
    all_rows = mu_index.shape[0]
    nsecond = ao_irrep.shape[0]
    slab_coeff = lax.dynamic_slice_in_dim(coeff, lax.axis_index("grp") * slab, slab, 0)
    rows_first = integrals.transpose(1, 0, 2).reshape(slab * rows_dev, nbasis)
    quarter = jnp.dot(rows_first, coeff, preferred_element_type=F32)
    quarter = quarter.astype(BF16).reshape(slab, rows_dev, nactive)
    partial_value = jnp.einsum("lp,lrq->rpq", slab_coeff, quarter, preferred_element_type=F32)
    partial_value = partial_value.reshape(rows_dev, total)
    mine = lax.psum_scatter(partial_value, "grp", scatter_dimension=1, tiled=True)
    picked = jnp.take(coeff, mu_index, axis=0).astype(F32)
    onehot = (nu_index[:, None] == jnp.arange(nsecond, dtype=jnp.int32)[None, :]).astype(F32)
    amat = (onehot[:, :, None] * picked[:, None, :]).reshape(all_rows, nsecond * nactive)
    sectioned = mine.reshape(rows_dev, owners, subset)
    arrived = lax.all_to_all(sectioned, "pair", split_axis=1, concat_axis=0, tiled=True)
    flat = arrived.reshape(all_rows, arrived.shape[2])
    full = lax.dot_general(flat, amat, (((0,), (0,)), ((), ())), precision=lax.Precision.HIGHEST)
    block_id = lax.axis_index("grp") * owners + lax.axis_index("pair")
    pair_ids = block_id * subset + jnp.arange(subset, dtype=jnp.int32)
    left_irrep = jnp.bitwise_xor(
        jnp.take(act_irrep, pair_ids // nactive), jnp.take(act_irrep, pair_ids % nactive)
    )
    col_ids = jnp.arange(nsecond * nactive, dtype=jnp.int32)
    right_irrep = jnp.bitwise_xor(
        jnp.take(ao_irrep, col_ids // nactive), jnp.take(act_irrep, col_ids % nactive)
    )
    allowed = left_irrep[:, None] == right_irrep[None, :]
    return jnp.where(allowed, full, jnp.zeros_like(full))


def section_of(shape, nactive, nsecond):
    col = lax.broadcasted_iota(jnp.int32, shape, 1)
    section = jnp.zeros(shape, jnp.int32)
    for n in range(1, nsecond):
        section = section + jnp.where(col >= n * nactive, 1, 0)
    return section


def transform_kernel(
    dims, x_hbm, c_hbm, mu_hbm, nu_hbm, ao_hbm, act_hbm, flat_hbm, amat_hbm, right_hbm, act_out,
    xv, cv, st, cpad, c32, qv, pv, muv, nuv, aov, actv, from_core, kept, from_y, summed, flat,
    picked, nu_col, amat_ref, right_ref, act_col, out_sem, x_sem, in_sem, core_send, core_recv, y_send, y_recv, pair_send, pair_recv,
):
    groups, owners, slab, rows_dev, nbasis, nact, nsecond, all_rows, chunk, early = dims
    layers = groups // 2
    per_group = nact // groups
    per_owner = per_group // owners
    grows = per_group * rows_dev
    orows = per_owner * rows_dev
    g = lax.axis_index("grp")
    me = lax.axis_index("pair")
    y, core = g // 2, g % 2
    other = 1 - core
    nchunks = slab * rows_dev // chunk

    small = [
        pltpu.make_async_copy(src, dst, in_sem.at[k])
        for k, (src, dst) in enumerate(
            ((c_hbm, cv.at[pl.ds(0, nact), :]), (mu_hbm, muv), (nu_hbm, nuv), (ao_hbm, aov), (act_hbm, actv))
        )
    ]
    small[0].start()

    def x_copy(k):
        where = pl.ds(pl.multiple_of(k * chunk, 16), chunk)
        return pltpu.make_async_copy(x_hbm.at[where, :], xv.at[where, :], x_sem.at[k])

    for k in range(min(AHEAD, nchunks)):
        x_copy(k).start()
    for copy in small[1:]:
        copy.start()

    barrier = pltpu.get_barrier_semaphore()
    pl.semaphore_signal(barrier, inc=1, device_id=(y * 2 + other, me), device_id_type=MESH)
    for d in range(1, layers):
        yy = lax.rem(y + d, layers)
        pl.semaphore_signal(barrier, inc=1, device_id=(yy * 2 + core, me), device_id_type=MESH)
    for d in range(1, owners):
        pl.semaphore_signal(
            barrier, inc=1, device_id=(g, lax.rem(me + d, owners)), device_id_type=MESH
        )

    cv[nact:, :] = jnp.zeros((LANES - nact, nbasis), BF16)
    small[0].wait()
    cpad[...] = cv[...].T


    def quarter_step(k, carry):
        x_copy(k).wait()

        @pl.when(k + AHEAD < nchunks)
        def _():
            x_copy(k + AHEAD).start()

        where = pl.ds(pl.multiple_of(k * chunk, 16), chunk)
        qv[where, :] = jnp.dot(xv[where, :], cpad[...], preferred_element_type=F32)
        return carry

    def half_part(first, count, fresh):
        for i in range(0, rows_dev, 2):
            q = jnp.concatenate(
                [
                    qv[pl.ds(first * rows_dev + i + k, count, stride=rows_dev), :].astype(BF16)
                    for k in range(2)
                ],
                axis=1,
            )
            part = jnp.dot(st[:, first : first + count], q, preferred_element_type=F32)
            for k in range(2):
                spot = pl.ds(i + k, nact, stride=rows_dev)
                mine = part[:, k * LANES : (k + 1) * LANES]
                pv[spot, :] = mine if fresh else pv[spot, :] + mine

    lax.fori_loop(0, early, quarter_step, 0)
    for part in range(groups):

        @pl.when(g == part)
        def _():
            st[:, :slab] = cv[:nact, part * slab : (part + 1) * slab]

    cut = early * chunk // rows_dev // 256 * 256
    if cut:
        half_part(0, cut, True)
    lax.fori_loop(early, nchunks, quarter_step, 0)
    half_part(cut, slab - cut, not cut)

    pl.semaphore_wait(barrier, layers + owners - 1)

    steps = owners // 2
    srows = 2 * orows

    def spot_of(step):
        b = lax.rem(me // 2 + steps // 2 + step, steps)
        return b, pl.multiple_of(b * srows, 8)

    def core_copy(d, step):
        layer = lax.rem(y + d, layers)
        _, at = spot_of(step)
        src = pl.multiple_of((layer * 2 + other) * grows + at, 8)
        return pltpu.make_async_remote_copy(
            src_ref=pv.at[pl.ds(src, srows), :],
            dst_ref=from_core.at[d, pl.ds(at, srows), :],
            send_sem=core_send.at[d, step],
            recv_sem=core_recv.at[d, step],
            device_id=(y * 2 + other, me),
            device_id_type=MESH,
        )

    def y_copy(d, step):
        layer = lax.rem(y + d, layers)
        _, at = spot_of(step)
        return pltpu.make_async_remote_copy(
            src_ref=kept.at[d, pl.ds(at, srows), :],
            dst_ref=from_y.at[d - 1, pl.ds(at, srows), :],
            send_sem=y_send.at[d - 1, step],
            recv_sem=y_recv.at[d - 1, step],
            device_id=(layer * 2 + core, me),
            device_id_type=MESH,
        )

    def pair_copy(d):
        to = lax.rem(me + d, owners)
        return pltpu.make_async_remote_copy(
            src_ref=summed.at[pl.ds(pl.multiple_of(to * orows, 8), orows), :],
            dst_ref=flat.at[pl.ds(pl.multiple_of(me * orows, 8), orows), :],
            send_sem=pair_send.at[d],
            recv_sem=pair_recv.at[d],
            device_id=(g, to),
            device_id_type=MESH,
        )

    order = list(range(1, layers)) + [0]
    for d in order:
        for step in range(steps):
            core_copy(d, step).start()
    for d in order:
        for step in range(steps):
            core_copy(d, step).wait_recv()
            _, at = spot_of(step)
            layer = lax.rem(y + d, layers)
            src = pl.multiple_of((layer * 2 + core) * grows + at, 8)
            here = pl.ds(at, srows)
            kept[d, here, :] = pv[pl.ds(src, srows), :] + from_core[d, here, :]
            if d:
                y_copy(d, step).start()

    for step in range(steps):
        b, at = spot_of(step)
        here = pl.ds(at, srows)
        total = kept[0, here, :]
        for d in range(1, layers):
            y_copy(d, step).wait_recv()
            total = total + from_y[d - 1, here, :]
        summed[here, :] = total
        for half in range(2):
            to = b * 2 + half

            @pl.when(to != me)
            def _():
                gap = lax.rem(to - me + owners, owners)
                pair_copy(gap).start()

    own = pl.ds(pl.multiple_of(me * orows, 8), orows)
    flat[own, :] = summed[own, :]
    for copy in small[1:]:
        copy.wait()
    cols = nsecond * nact
    c32[...] = cpad[...].astype(F32)

    def pick_row(i, carry):
        picked[pl.ds(i, 1), :] = c32[pl.ds(muv[i], 1), :]
        nu_col[pl.ds(i, 1), :] = jnp.broadcast_to(nuv[i], (1, LANES))
        return carry

    def act_row(i, carry):
        act_col[pl.ds(i, 1), :] = jnp.broadcast_to(actv[i], (1, LANES))
        return carry

    lax.fori_loop(0, all_rows, pick_row, 0)
    lax.fori_loop(0, nact, act_row, 0)
    section = section_of((1, cols), nact, nsecond)
    inside = lax.broadcasted_iota(jnp.int32, (1, cols), 1) - section * nact
    spread = inside == lax.broadcasted_iota(jnp.int32, (nact, cols), 0)
    wide = jnp.dot(
        picked[:, :nact].astype(BF16),
        jnp.where(spread, 1.0, 0.0).astype(BF16),
        preferred_element_type=F32,
    )
    amat_ref[...] = jnp.where(section == nu_col[:, :1], wide, 0.0).astype(BF16)
    act_wide = jnp.sum(
        jnp.where(spread, act_col[:, :1].astype(F32), 0.0), axis=0, keepdims=True
    ).astype(jnp.int32)
    ao_wide = jnp.zeros((1, cols), jnp.int32)
    for n in range(nsecond):
        ao_wide = jnp.where(section == n, aov[n], ao_wide)
    right_ref[...] = jnp.broadcast_to(jnp.bitwise_xor(act_wide, ao_wide), (8, cols))
    results = [
        pltpu.make_async_copy(src, dst, out_sem.at[k])
        for k, (src, dst) in enumerate(
            (
                (flat, flat_hbm),
                (amat_ref, amat_hbm),
                (right_ref, right_hbm),
                (act_col, act_out),
            )
        )
    ]
    for copy in results[1:]:
        copy.start()

    for d in range(1, owners):
        pair_copy(d).wait_recv()
    results[0].start()
    for d in order:
        for step in range(steps):
            core_copy(d, step).wait_send()
            if d:
                y_copy(d, step).wait_send()
    for d in range(1, owners):
        pair_copy(d).wait_send()
    for copy in results:
        copy.wait()


def finish_kernel(
    dims, flat_hbm, amat_hbm, right_hbm, act_in, out_hbm,
    flat, amat_ref, right_ref, act_col, out, in_sem, out_sem,
):
    owners, rows_dev, per_owner, nact = dims
    first = (lax.axis_index("grp") * owners + lax.axis_index("pair")) * per_owner
    arrived = [
        pltpu.make_async_copy(src, dst, in_sem.at[k])
        for k, (src, dst) in enumerate(
            (
                (flat_hbm, flat),
                (amat_hbm, amat_ref),
                (right_hbm, right_ref),
                (act_in, act_col),
            )
        )
    ]
    for copy in arrived:
        copy.start()
    for copy in arrived:
        copy.wait()
    weights = jnp.concatenate([amat_ref[...]] * 3, axis=0)
    right = right_ref[:1, :]
    copies = []
    for j in range(per_owner):
        f = jnp.concatenate(
            [
                flat[pl.ds((s * per_owner + j) * rows_dev, rows_dev), :]
                for s in range(owners)
            ],
            axis=0,
        )
        high = f.astype(BF16)
        rest = f - high.astype(F32)
        mid = rest.astype(BF16)
        low = (rest - mid.astype(F32)).astype(BF16)
        parts = jnp.concatenate([high, mid, low], axis=0).astype(F32).T[:nact].astype(BF16)
        full = jnp.dot(parts, weights, preferred_element_type=F32)
        p = first + j
        left = jnp.bitwise_xor(act_col[:, :1], act_col[pl.ds(p, 1), :1])
        here = pl.ds(j * nact, nact)
        out[here, :] = jnp.where(left == right, full, 0.0)
        copies.append(pltpu.make_async_copy(out.at[here, :], out_hbm.at[here, :], out_sem.at[j]))
        copies[-1].start()
    for copy in copies:
        copy.wait()


def fast(integrals, coeff, mu_index, nu_index, ao_irrep, act_irrep):
    rows_dev, slab, nbasis = integrals.shape
    nact = coeff.shape[1]
    groups, owners = lax.axis_size("grp"), lax.axis_size("pair")
    all_rows, nsecond = mu_index.shape[0], ao_irrep.shape[0]
    layers = groups // 2
    per_owner = nact // groups // owners
    grows = nact // groups * rows_dev
    cols = nsecond * nact
    rows = slab * rows_dev
    chunk = max(c for c in range(16, 401, 16) if rows % c == 0)
    nchunks = rows // chunk
    early = min(nchunks, -(-256 * rows_dev // chunk))
    dims = (groups, owners, slab, rows_dev, nbasis, nact, nsecond, all_rows, chunk, early)
    span = -(-slab // 256) * 256
    x = integrals.transpose(1, 0, 2).reshape(rows, nbasis)
    steps = owners // 2
    hbm = pl.BlockSpec(memory_space=pltpu.HBM)
    tables = pl.pallas_call(
        functools.partial(transform_kernel, dims),
        out_shape=(
            jax.ShapeDtypeStruct((grows, LANES), F32),
            jax.ShapeDtypeStruct((all_rows, cols), BF16),
            jax.ShapeDtypeStruct((8, cols), jnp.int32),
            jax.ShapeDtypeStruct((nact, LANES), jnp.int32),
        ),
        in_specs=[hbm] * 6,
        out_specs=(hbm,) * 4,
        scratch_shapes=[
            pltpu.VMEM((rows, nbasis), BF16),
            pltpu.VMEM((LANES, nbasis), BF16),
            pltpu.VMEM((nact, span), BF16),
            pltpu.VMEM((nbasis, LANES), BF16),
            pltpu.VMEM((nbasis, LANES), F32),
            pltpu.VMEM((rows, LANES), F32),
            pltpu.VMEM((nact * rows_dev, LANES), F32),
            pltpu.SMEM((all_rows,), jnp.int32),
            pltpu.SMEM((all_rows,), jnp.int32),
            pltpu.SMEM((nsecond,), jnp.int32),
            pltpu.SMEM((nact,), jnp.int32),
            pltpu.VMEM((layers, grows, LANES), F32),
            pltpu.VMEM((layers, grows, LANES), F32),
            pltpu.VMEM((layers - 1, grows, LANES), F32),
            pltpu.VMEM((grows, LANES), F32),
            pltpu.VMEM((grows, LANES), F32),
            pltpu.VMEM((all_rows, LANES), F32),
            pltpu.VMEM((all_rows, LANES), jnp.int32),
            pltpu.VMEM((all_rows, cols), BF16),
            pltpu.VMEM((8, cols), jnp.int32),
            pltpu.VMEM((nact, LANES), jnp.int32),
            pltpu.SemaphoreType.DMA((4,)),
            pltpu.SemaphoreType.DMA((nchunks,)),
            pltpu.SemaphoreType.DMA((5,)),
            pltpu.SemaphoreType.DMA((layers, steps)),
            pltpu.SemaphoreType.DMA((layers, steps)),
            pltpu.SemaphoreType.DMA((layers - 1, steps)),
            pltpu.SemaphoreType.DMA((layers - 1, steps)),
            pltpu.SemaphoreType.DMA((owners,)),
            pltpu.SemaphoreType.DMA((owners,)),
        ],
        compiler_params=pltpu.CompilerParams(
            collective_id=0, has_side_effects=True, vmem_limit_bytes=VMEM_LIMIT
        ),
        cost_estimate=pl.CostEstimate(
            flops=2 * rows * nbasis * nact, bytes_accessed=rows * nbasis * 2, transcendentals=0
        ),
    )(x, coeff.T, mu_index, nu_index, ao_irrep, act_irrep)
    return pl.pallas_call(
        functools.partial(finish_kernel, (owners, rows_dev, per_owner, nact)),
        out_shape=jax.ShapeDtypeStruct((per_owner * nact, cols), F32),
        in_specs=[hbm] * 4,
        out_specs=hbm,
        scratch_shapes=[
            pltpu.VMEM((grows, LANES), F32),
            pltpu.VMEM((all_rows, cols), BF16),
            pltpu.VMEM((8, cols), jnp.int32),
            pltpu.VMEM((nact, LANES), jnp.int32),
            pltpu.VMEM((per_owner * nact, cols), F32),
            pltpu.SemaphoreType.DMA((4,)),
            pltpu.SemaphoreType.DMA((per_owner,)),
        ],
        compiler_params=pltpu.CompilerParams(vmem_limit_bytes=VMEM_LIMIT),
    )(*tables)


def on_device(integrals, coeff, mu_index, nu_index, ao_irrep, act_irrep):
    rows_dev, slab, _ = integrals.shape
    nact = coeff.shape[1]
    groups, owners = lax.axis_size("grp"), lax.axis_size("pair")
    whole_rows = nact % (groups * owners) == 0
    fits = rows_dev == 8 and groups % 2 == 0 and groups > 2 and owners % 2 == 0
    if whole_rows and fits and slab * rows_dev % 16 == 0 and nact <= LANES:
        return fast(integrals, coeff, mu_index, nu_index, ao_irrep, act_irrep)
    return generic(integrals, coeff, mu_index, nu_index, ao_irrep, act_irrep)


def solution(mesh):
    in_specs = (P("pair", "grp", None), P(), P(), P(), P(), P())
    out_specs = P(("grp", "pair"), None)
    return jax.shard_map(
        on_device, mesh=mesh, in_specs=in_specs, out_specs=out_specs, check_vma=False
    )
```
